32 devices in a mesh: leaf: 8 (over y, x, core), front: 4 (over z).
Axes of the slice: x: 2, y: 2, z: 4, core: 2. Of those that a mesh axis runs over, the one named last changes fastest.
Arguments:
- leaf_contrib: float32 [8192, 1024], P(('leaf', 'front')), may hold values from -1 to 7, as said below
- entries_lower: float32 [8192, 1024], P(('leaf', 'front')), may hold values from -1 to 4, as said below
- entries_middle: float32 [4096, 1024], P(('leaf', 'front')), may hold values from -1 to 4, as said below
- entries_upper: float32 [2048, 1024], P(('leaf', 'front')), may hold values from -1 to 4, as said below
- assembly_lower: int32 [4, 2, 8], replicated, may hold values from 0 to 15, as said below
- assembly_middle: int32 [2, 2, 8], replicated, may hold values from 0 to 15, as said below
- assembly_upper: int32 [1, 2, 8], replicated, may hold values from 0 to 15, as said below
Outputs:
- factor_lower: float32 [8192, 1024], P(('leaf', 'front'))
- factor_middle: float32 [4096, 1024], P(('leaf', 'front'))
- factor_upper: float32 [2048, 1024], P(('leaf', 'front'))
- top_update: float32 [1024, 1024], P(('leaf', 'front'))
The draws below stay inside these ranges and needn't reach their ends.
Inputs may be any that keep to these rules, and one draw needn't show every extreme that they name: `leaf_contrib`: in natural row order each leaf's block is symmetric positive definite. `entries_lower`: in natural row order the first 1024 rows of each front's entries form a symmetric positive definite block. `entries_middle`: in natural row order the first 1024 rows of each front's entries form a symmetric positive definite block. `entries_upper`: in natural row order the first 1024 rows of each front's entries form a symmetric positive definite block. `assembly_lower`: each child's block j goes to parent block j or j + 8, and at least one of the two children sends its block j to j + 8. `assembly_middle`: each child's block j goes to parent block j or j + 8, and at least one of the two children sends its block j to j + 8. `assembly_upper`: each child's block j goes to parent block j or j + 8, and at least one of the two children sends its block j to j + 8.
All inputs are finite; a program needn't handle non-finite values.
Results may differ from the reference program's by a relative error of at most 0.0003.
Values sent between devices are 32-bit elements; how exact they have to be, the bound alone decides.
No kernel may reach another device: no remote copies, remote signals or barrier semaphores. Data moves between devices by JAX's collectives and lax.ppermute only.
A program may use at most 128 MiB of HBM per device.

```python
import math
import jax
import jax.numpy as jnp
import numpy as np
from jax import lax

BLK = 128
PIVOT_BLOCKS = 8
LEVELS = 3
PIVOT = 1024
FRONT = 2048
LOCAL_BLOCKS = 2
FRONTS_LOWER = 4
FRONTS_MIDDLE = 2
FRONTS_UPPER = 1
N_LEAF = 8


def bit_reverse_drawn(number, bit_count):
    result = 0
    for bit_index in range(bit_count):
        result = result | (number >> bit_index & 1) << bit_count - 1 - bit_index
    return result


def stored_rows(height, update_only):
    groups = 2 ** height
    piece_rows = BLK // groups
    front_devs = PIVOT_BLOCKS // LOCAL_BLOCKS
    portions = (1,) if update_only else (0, 1)
    row_list = []
    for member in range(groups):
        for front_dev in range(front_devs):
            for portion in portions:
                for local_block in range(LOCAL_BLOCKS):
                    block_index = front_dev + front_devs * local_block
                    if not update_only:
                        block_index = block_index + portion * PIVOT_BLOCKS
                    first_row = block_index * BLK + bit_reverse_drawn(member, height) * piece_rows
                    row_list.extend(range(first_row, first_row + piece_rows))
    return np.array(row_list, dtype=np.int32)


def symmetric_noise(noise_key, count, order_size):
    noise = jax.random.uniform(noise_key, (count, order_size, order_size), jnp.float32, -1.0, 1.0)
    return (noise + jnp.swapaxes(noise, 1, 2)) * (0.5 / math.sqrt(order_size))


def coupling_term(coupling_key, count, order_size):
    vector = jax.random.uniform(coupling_key, (count, order_size), jnp.float32, 0.0, 1.0)
    return 0.5 * vector[:, :, None] * vector[:, None, :]


def draw_leaf_contrib(key, part):
    key = jax.random.fold_in(key, 7)
    noise_key = jax.random.fold_in(key, 0)
    diag_key = jax.random.fold_in(key, 1)
    coupling_key = jax.random.fold_in(key, 3)
    matrix = symmetric_noise(noise_key, N_LEAF, PIVOT)
    diagonal = jax.random.uniform(diag_key, (N_LEAF, PIVOT), jnp.float32, 3.0, 4.5)
    matrix = matrix + diagonal[:, :, None] * jnp.eye(PIVOT, dtype=jnp.float32)[None]
    matrix = matrix + coupling_term(coupling_key, N_LEAF, PIVOT)
    return matrix[:, stored_rows(0, True)].reshape(N_LEAF * PIVOT, PIVOT)


def entries_draw(key, fronts, height):
    noise_key = jax.random.fold_in(key, 0)
    diag_key = jax.random.fold_in(key, 1)
    lower_key = jax.random.fold_in(key, 2)
    coupling_key = jax.random.fold_in(key, 4)
    pivot_part = symmetric_noise(noise_key, fronts, PIVOT)
    spread = jax.random.uniform(diag_key, (fronts, PIVOT), jnp.float32, 0.0, 1.0)
    diagonal = 1.3 + 1.3 * spread
    pivot_part = pivot_part + diagonal[:, :, None] * jnp.eye(PIVOT, dtype=jnp.float32)[None]
    pivot_part = pivot_part + coupling_term(coupling_key, fronts, PIVOT)
    update_part = jax.random.uniform(lower_key, (fronts, PIVOT, PIVOT), jnp.float32, -1.0, 1.0) * (0.55 / math.sqrt(PIVOT))
    matrix = jnp.concatenate([pivot_part, update_part], axis=1)
    return matrix[:, stored_rows(height, False)].reshape(fronts * FRONT, PIVOT)


def draw_entries_lower(key, part):
    return entries_draw(jax.random.fold_in(key, 11), FRONTS_LOWER, 1)


def draw_entries_middle(key, part):
    return entries_draw(jax.random.fold_in(key, 12), FRONTS_MIDDLE, 2)


def draw_entries_upper(key, part):
    return entries_draw(jax.random.fold_in(key, 13), FRONTS_UPPER, 3)


def assembly_draw(key, fronts):
    choice_key, force_key = jax.random.split(key)
    selection = jax.random.randint(choice_key, (fronts, PIVOT_BLOCKS), 0, 3, dtype=jnp.int32)
    forced = 1 + jax.random.randint(force_key, (fronts, PIVOT_BLOCKS), 0, 2, dtype=jnp.int32)
    first_cell = (jnp.arange(fronts)[:, None] == 0) & (jnp.arange(PIVOT_BLOCKS)[None, :] == 0)
    selection = jnp.where(first_cell, forced, selection)
    blocks = jnp.arange(PIVOT_BLOCKS, dtype=jnp.int32)[None, :]
    first_child = blocks + PIVOT_BLOCKS * (selection != 1).astype(jnp.int32)
    second_child = blocks + PIVOT_BLOCKS * (selection != 2).astype(jnp.int32)
    return jnp.stack([first_child, second_child], axis=1).astype(jnp.int32)


def draw_assembly_lower(key, part):
    return assembly_draw(jax.random.fold_in(key, 21), FRONTS_LOWER)


def draw_assembly_middle(key, part):
    return assembly_draw(jax.random.fold_in(key, 22), FRONTS_MIDDLE)


def draw_assembly_upper(key, part):
    return assembly_draw(jax.random.fold_in(key, 23), FRONTS_UPPER)


def setup_inputs(seed: int = 0) -> dict:
    key_list = jax.random.split(jax.random.key(seed), 8)
    leaf_contrib = draw_leaf_contrib(jax.random.fold_in(key_list[7], 71), 0)
    entries_lower = draw_entries_lower(jax.random.fold_in(key_list[7], 71), 0)
    entries_middle = draw_entries_middle(jax.random.fold_in(key_list[7], 71), 0)
    entries_upper = draw_entries_upper(jax.random.fold_in(key_list[7], 71), 0)
    assembly_lower = draw_assembly_lower(jax.random.fold_in(key_list[7], 71), 0)
    assembly_middle = draw_assembly_middle(jax.random.fold_in(key_list[7], 71), 0)
    assembly_upper = draw_assembly_upper(jax.random.fold_in(key_list[7], 71), 0)
    return dict(leaf_contrib=leaf_contrib, entries_lower=entries_lower, entries_middle=entries_middle, entries_upper=entries_upper, assembly_lower=assembly_lower, assembly_middle=assembly_middle, assembly_upper=assembly_upper)


def bit_reverse(number, bit_count):
    result = 0
    for bit_index in range(bit_count):
        result = result | (number >> bit_index & 1) << bit_count - 1 - bit_index
    return result

def natural_rows(height, update_only):
    groups = 2 ** height
    piece_rows = BLK // groups
    front_devs = PIVOT_BLOCKS // LOCAL_BLOCKS
    portions = (1,) if update_only else (0, 1)
    row_list = []
    for member in range(groups):
        for front_dev in range(front_devs):
            for portion in portions:
                for local_block in range(LOCAL_BLOCKS):
                    block_index = front_dev + front_devs * local_block
                    if not update_only:
                        block_index = block_index + portion * PIVOT_BLOCKS
                    first_row = block_index * BLK + bit_reverse(member, height) * piece_rows
                    row_list.extend(range(first_row, first_row + piece_rows))
    return np.array(row_list, dtype=np.int32)

def assemble(entries, first_child, second_child, routes):
    matrix = jnp.zeros((FRONT, FRONT), jnp.float32)
    matrix = matrix.at[:, :PIVOT].set(entries)
    matrix = matrix.at[:PIVOT, PIVOT:].set(entries[PIVOT:].T)
    offsets = jnp.arange(BLK, dtype=jnp.int32)
    for child_index, child_block in ((0, first_child), (1, second_child)):
        places = (routes[child_index][:, None] * BLK + offsets[None, :]).reshape(-1).astype(jnp.int32)
        matrix = matrix.at[places[:, None], places[None, :]].add(child_block)
    return matrix

def factor_front(operands):
    entries, first_child, second_child, routes = operands
    matrix = assemble(entries, first_child, second_child, routes)
    lower_factor = jnp.linalg.cholesky(matrix[:PIVOT, :PIVOT])
    panel_rows = jax.scipy.linalg.solve_triangular(lower_factor, matrix[PIVOT:, :PIVOT].T, lower=True).T
    schur_block = matrix[PIVOT:, PIVOT:] - jnp.dot(panel_rows.astype(jnp.float32), panel_rows.T.astype(jnp.float32), precision=lax.Precision.HIGHEST, preferred_element_type=jnp.float32)
    return (jnp.concatenate([lower_factor, panel_rows], axis=0), schur_block)

def reference(leaf_contrib, entries_lower, entries_middle, entries_upper, assembly_lower, assembly_middle, assembly_upper):
    leaf_order = natural_rows(0, True)
    contrib = leaf_contrib.reshape(N_LEAF, PIVOT, PIVOT)[:, np.argsort(leaf_order)]
    outputs = []
    for height, entries, routes in ((1, entries_lower, assembly_lower), (2, entries_middle, assembly_middle), (3, entries_upper, assembly_upper)):
        fronts = N_LEAF // 2 ** height
        row_order = natural_rows(height, False)
        natural_entries = entries.reshape(fronts, FRONT, PIVOT)[:, np.argsort(row_order)]
        children = contrib.reshape(fronts, 2, PIVOT, PIVOT)
        factors, contrib = lax.map(factor_front, (natural_entries, children[:, 0], children[:, 1], routes))
        outputs.append(factors[:, row_order].reshape(fronts * FRONT, PIVOT))
    top_order = natural_rows(LEVELS, True)
    top_update = contrib[:, top_order].reshape(-1, PIVOT)
    return (outputs[0], outputs[1], outputs[2], top_update)
```

```python
import jax
import jax.numpy as jnp
from jax import lax
from jax.experimental import pallas as pl
from jax.experimental.pallas import tpu as pltpu
from jax.sharding import PartitionSpec as P

BLK = 128
PIVOT_BLOCKS = 8
SUB = 8


def split_parts(value):
    high = value.astype(jnp.bfloat16)
    low = (value - high.astype(jnp.float32)).astype(jnp.bfloat16)
    return high, low


def product_3(left, right, transposed=False):
    dims = (((1,), (1 if transposed else 0,)), ((), ()))
    left_high, left_low = split_parts(left)
    right_high, right_low = split_parts(right)

    def one(first, second):
        return lax.dot_general(first, second, dims, preferred_element_type=jnp.float32)

    return one(left_high, right_high) + (one(left_high, right_low) + one(left_low, right_high))


def invert_block(block, inverse_ref):
    count = BLK // SUB
    shape = (SUB, BLK)
    rows = [block[SUB * m : SUB * m + SUB] for m in range(count)]
    lane = lax.broadcasted_iota(jnp.int32, shape, 1)
    sublane = lax.broadcasted_iota(jnp.int32, shape, 0)
    unit = [(lane == sublane + SUB * m).astype(jnp.float32) for m in range(count)]
    for k in range(count):
        base = SUB * k
        cols = [jnp.broadcast_to(rows[k][:, base + j : base + j + 1], shape) for j in range(SUB)]
        d = [[jnp.broadcast_to(cols[j][i : i + 1], shape) for j in range(i + 1)] for i in range(SUB)]
        ya = [jnp.broadcast_to(rows[k][j : j + 1], shape) for j in range(SUB)]
        ye = [jnp.broadcast_to(unit[k][j : j + 1], shape) for j in range(SUB)]
        f = [[None] * SUB for _ in range(SUB)]
        reciprocal = [None] * SUB
        for c in range(SUB):
            reciprocal[c] = 1.0 / d[c][c]
            for i in range(c + 1, SUB):
                f[i][c] = d[i][c] * reciprocal[c]
            for i in range(c + 1, SUB):
                for j in range(c + 1, i + 1):
                    d[i][j] = d[i][j] - (d[i][c] * d[j][c]) * reciprocal[c]
            for i in range(c + 1, SUB):
                ya[i] = ya[i] - f[i][c] * ya[c]
                ye[i] = ye[i] - f[i][c] * ye[c]
            inverse_ref[base + c : base + c + 1, :] = (lax.rsqrt(d[c][c]) * ye[c])[0:1]
        if k == count - 1:
            break
        za = [y * r for y, r in zip(ya, reciprocal)]
        ze = [y * r for y, r in zip(ye, reciprocal)]
        for i in reversed(range(SUB)):
            for c in range(i):
                za[c] = za[c] - f[i][c] * za[i]
                ze[c] = ze[c] - f[i][c] * ze[i]
        for m in range(k + 1, count):
            col = [jnp.broadcast_to(rows[m][:, base + j : base + j + 1], shape) for j in range(SUB)]
            pa = [c * z for c, z in zip(col, za)]
            pe = [c * z for c, z in zip(col, ze)]
            while len(pa) > 1:
                pa = [x + y for x, y in zip(pa[::2], pa[1::2])]
                pe = [x + y for x, y in zip(pe[::2], pe[1::2])]
            rows[m] = rows[m] - pa[0]
            unit[m] = unit[m] - pe[0]


def factor_kernel(matrix_ref, factor_ref, inverse_ref, work_ref, block_ref):
    size = matrix_ref.shape[0]
    work_ref[:, :size] = matrix_ref[...]
    row = lax.broadcasted_iota(jnp.int32, (size, size), 0)
    column = lax.broadcasted_iota(jnp.int32, (size, size), 1)
    work_ref[:, size:] = (row == column).astype(jnp.float32)
    row = lax.broadcasted_iota(jnp.int32, (size, BLK), 0)
    column = lax.broadcasted_iota(jnp.int32, (size, BLK), 1)

    def step(index, carry):
        base = pl.multiple_of(index * BLK, BLK)
        invert_block(work_ref[pl.ds(base, BLK), pl.ds(base, BLK)], block_ref)
        block = block_ref[...]
        below = product_3(work_ref[:, pl.ds(base, BLK)], block, transposed=True)
        right = product_3(block, work_ref[pl.ds(base, BLK), :])
        below = jnp.where(row >= column + base, below, 0.0)
        factor_ref[:, pl.ds(base, BLK)] = below
        inverse_ref[pl.ds(base, BLK), :] = right[:, size:]
        below = jnp.where(row >= base + BLK, below, 0.0)
        work_ref[...] = work_ref[...] - product_3(below, right)
        return carry

    lax.fori_loop(0, size // BLK, step, 0)


def factor_inverse(matrix):
    size = matrix.shape[0]
    vmem = pl.BlockSpec(memory_space=pltpu.VMEM)
    whole = jax.ShapeDtypeStruct((size, size), jnp.float32)
    return pl.pallas_call(
        factor_kernel,
        out_shape=[whole, whole],
        in_specs=[vmem],
        out_specs=[vmem, vmem],
        scratch_shapes=[
            pltpu.VMEM((size, 2 * size), jnp.float32),
            pltpu.VMEM((BLK, BLK), jnp.float32),
        ],
        compiler_params=pltpu.CompilerParams(vmem_limit_bytes=48 * 2**20),
        cost_estimate=pl.CostEstimate(
            flops=60_000_000_000 * size // 1024, bytes_accessed=12 * size * size, transcendentals=0
        ),
        name="factor_inverse",
    )(matrix)


def partner_2(value, axis, stride):
    mask = 2**stride
    pairs = [(source, source ^ mask) for source in range(lax.axis_size(axis))]
    return lax.ppermute(value, axis, pairs)


def product(left, right):
    return jnp.dot(left, right, precision=lax.Precision.HIGH, preferred_element_type=jnp.float32)


def reversed_bits(number, bit_count):
    result = jnp.zeros((), jnp.int32)
    for bit_index in range(bit_count):
        result = result + (number >> bit_index & 1) * (1 << bit_count - 1 - bit_index)
    return result


def join_pieces(mine, theirs, bit_index):
    upper_bit = lax.axis_index("leaf") >> bit_index & 1
    return jnp.where(
        upper_bit == 0,
        jnp.concatenate([mine, theirs], 1),
        jnp.concatenate([theirs, mine], 1),
    )


def group_gather(pieces, height):
    gathered = lax.all_gather(pieces, "front", axis=0, tiled=False)
    for bit_index in reversed(range(height)):
        partner = partner_2(gathered, "leaf", bit_index)
        gathered = join_pieces(gathered, partner, bit_index)
    return gathered.reshape(-1, pieces.shape[-1])


def spread_columns(rows_in, upper_mask):
    blocks = rows_in.reshape(rows_in.shape[0], rows_in.shape[1], upper_mask.shape[0], -1)
    to_pivot = blocks * (1.0 - upper_mask)[None, None, :, None]
    to_update = blocks * upper_mask[None, None, :, None]
    return jnp.concatenate([to_pivot, to_update], axis=2).reshape(
        rows_in.shape[0], rows_in.shape[1], -1
    )


def own_rows(whole, front_index, piece_index, piece_rows):
    chosen = lax.dynamic_index_in_dim(whole, front_index, 1, keepdims=False)
    return lax.dynamic_slice_in_dim(chosen, piece_index * piece_rows, piece_rows, 1)


def solve_panel(rows, chunk, factors, inverses):
    panels = []
    for index, inverse in enumerate(inverses):
        part = rows[:, index * chunk : (index + 1) * chunk]
        for previous in range(index):
            part = part - product(panels[previous], factors[index][previous].T)
        panels.append(product(part, inverse.T))
    return jnp.concatenate(panels, axis=1)


def local(
    leaf_contrib,
    entries_lower,
    entries_middle,
    entries_upper,
    assembly_lower,
    assembly_middle,
    assembly_upper,
):
    front_count = lax.axis_size("front")
    local_count = PIVOT_BLOCKS // front_count
    chunk = front_count * BLK
    leaf_index = lax.axis_index("leaf")
    front_index = lax.axis_index("front")
    pivot_size = leaf_contrib.shape[1]
    update = leaf_contrib.reshape(local_count, BLK, pivot_size)
    my_blocks = front_index + front_count * jnp.arange(local_count, dtype=jnp.int32)
    selector = (jnp.arange(PIVOT_BLOCKS, dtype=jnp.int32)[None, :] == my_blocks[:, None]).astype(
        jnp.float32
    )
    results = []
    for height, entries, routes in (
        (1, entries_lower, assembly_lower),
        (2, entries_middle, assembly_middle),
        (3, entries_upper, assembly_upper),
    ):
        piece_rows = BLK // 2**height
        child_bit = leaf_index >> height - 1 & 1
        low_rows = update[:, :piece_rows]
        high_rows = update[:, piece_rows:]
        kept = jnp.where(child_bit == 0, low_rows, high_rows)
        outgoing = jnp.where(child_bit == 0, high_rows, low_rows)
        received = partner_2(outgoing, "leaf", height - 1)
        route_pair = lax.dynamic_index_in_dim(routes, leaf_index >> height, 0, keepdims=False)
        upper_masks = (route_pair >= PIVOT_BLOCKS).astype(jnp.float32)
        own_mask = jnp.where(child_bit == 0, upper_masks[0], upper_masks[1])
        other_mask = jnp.where(child_bit == 0, upper_masks[1], upper_masks[0])
        slab_rows = local_count * piece_rows
        pivot_slab = entries[:slab_rows].reshape(local_count, piece_rows, pivot_size)
        update_slab = jnp.zeros((local_count, piece_rows, 2 * pivot_size), jnp.float32)
        update_slab = update_slab.at[:, :, :pivot_size].set(
            entries[slab_rows:].reshape(local_count, piece_rows, pivot_size)
        )
        for contribution, column_mask in ((kept, own_mask), (received, other_mask)):
            spread = spread_columns(contribution, column_mask)
            row_upper = jnp.sum(selector * column_mask[None, :], axis=1)
            pivot_slab = pivot_slab + (1.0 - row_upper)[:, None, None] * spread[:, :, :pivot_size]
            update_slab = update_slab + row_upper[:, None, None] * spread
        piece_index = reversed_bits(leaf_index & 2**height - 1, height)
        update_pivot = update_slab[:, :, :pivot_size]
        pivot_rows = [
            group_gather(pivot_slab[t, :, : (t + 1) * chunk], height) for t in range(local_count)
        ]
        update_rows = [group_gather(update_pivot[t], height) for t in range(local_count)]
        factors, inverses = [], []
        for t in range(local_count):
            row = []
            for s in range(t):
                part = pivot_rows[t][:, s * chunk : (s + 1) * chunk]
                for r in range(s):
                    part = part - product(row[r], factors[s][r].T)
                row.append(product(part, inverses[s].T))
            part = pivot_rows[t][:, t * chunk :]
            for s in range(t):
                part = part - product(row[s], row[s].T)
            factor, inverse = factor_inverse(part)
            row.append(factor)
            factors.append(row)
            inverses.append(inverse)
        own_panel = solve_panel(update_pivot.reshape(-1, pivot_size), chunk, factors, inverses)
        all_panel = solve_panel(jnp.concatenate(update_rows, 0), chunk, factors, inverses)
        lower_factor = jnp.stack(
            [
                jnp.concatenate(
                    row + [jnp.zeros((chunk, chunk), jnp.float32)] * (local_count - 1 - t), axis=1
                )
                for t, row in enumerate(factors)
            ]
        )
        own_factor = own_rows(
            lower_factor.reshape(local_count, front_count, BLK, pivot_size),
            front_index,
            piece_index,
            piece_rows,
        ).reshape(-1, pivot_size)
        results.append(jnp.concatenate([own_factor, own_panel], axis=0))
        schur_rows = update_slab[:, :, pivot_size:].reshape(-1, pivot_size) - product(
            own_panel, all_panel.T
        )
        update = schur_rows.reshape(local_count, piece_rows, pivot_size)
    return (results[0], results[1], results[2], update.reshape(-1, pivot_size))


def solution(mesh):
    spec = P(("leaf", "front"), None)
    return jax.shard_map(
        local,
        mesh=mesh,
        in_specs=(spec, spec, spec, spec, P(), P(), P()),
        out_specs=(spec, spec, spec, spec),
        check_vma=False,
    )
```

```python
import jax
import jax.numpy as jnp
from jax import lax
from jax.experimental import pallas as pl
from jax.experimental.pallas import tpu as pltpu
from jax.sharding import PartitionSpec as P

BLK = 128
PIVOT_BLOCKS = 8
SUB = 8
STRIP = 256


def split_parts(value):
    high = value.astype(jnp.bfloat16)
    low = (value - high.astype(jnp.float32)).astype(jnp.bfloat16)
    return high, low


def product_3(left, right, transposed=False):
    dims = (((1,), (1 if transposed else 0,)), ((), ()))
    left_high, left_low = split_parts(left)
    right_high, right_low = split_parts(right)

    def one(first, second):
        return lax.dot_general(first, second, dims, preferred_element_type=jnp.float32)

    return one(left_high, right_high) + (one(left_high, right_low) + one(left_low, right_high))


def invert_block(block, inverse_ref):
    count = BLK // SUB
    shape = (SUB, BLK)
    rows = [block[SUB * m : SUB * m + SUB] for m in range(count)]
    lane = lax.broadcasted_iota(jnp.int32, shape, 1)
    sublane = lax.broadcasted_iota(jnp.int32, shape, 0)
    unit = [(lane == sublane + SUB * m).astype(jnp.float32) for m in range(count)]
    for k in range(count):
        base = SUB * k
        cols = [jnp.broadcast_to(rows[k][:, base + j : base + j + 1], shape) for j in range(SUB)]
        d = [[jnp.broadcast_to(cols[j][i : i + 1], shape) for j in range(i + 1)] for i in range(SUB)]
        ya = [jnp.broadcast_to(rows[k][j : j + 1], shape) for j in range(SUB)]
        ye = [jnp.broadcast_to(unit[k][j : j + 1], shape) for j in range(SUB)]
        f = [[None] * SUB for _ in range(SUB)]
        reciprocal = [None] * SUB
        for c in range(SUB):
            reciprocal[c] = 1.0 / d[c][c]
            for i in range(c + 1, SUB):
                f[i][c] = d[i][c] * reciprocal[c]
            for i in range(c + 1, SUB):
                for j in range(c + 1, i + 1):
                    d[i][j] = d[i][j] - (d[i][c] * d[j][c]) * reciprocal[c]
            for i in range(c + 1, SUB):
                ya[i] = ya[i] - f[i][c] * ya[c]
                ye[i] = ye[i] - f[i][c] * ye[c]
            inverse_ref[base + c : base + c + 1, :] = (lax.rsqrt(d[c][c]) * ye[c])[0:1]
        if k == count - 1:
            break
        za = [y * r for y, r in zip(ya, reciprocal)]
        ze = [y * r for y, r in zip(ye, reciprocal)]
        for i in reversed(range(SUB)):
            for c in range(i):
                za[c] = za[c] - f[i][c] * za[i]
                ze[c] = ze[c] - f[i][c] * ze[i]
        for m in range(k + 1, count):
            col = [jnp.broadcast_to(rows[m][:, base + j : base + j + 1], shape) for j in range(SUB)]
            pa = [c * z for c, z in zip(col, za)]
            pe = [c * z for c, z in zip(col, ze)]
            while len(pa) > 1:
                pa = [x + y for x, y in zip(pa[::2], pa[1::2])]
                pe = [x + y for x, y in zip(pe[::2], pe[1::2])]
            rows[m] = rows[m] - pa[0]
            unit[m] = unit[m] - pe[0]


def factor_in_place(work_ref, block_ref, factor_ref, first_column, inverse_ref):
    size = work_ref.shape[0]
    row = lax.broadcasted_iota(jnp.int32, (size, size), 0)
    column = lax.broadcasted_iota(jnp.int32, (size, size), 1)
    work_ref[:, size:] = (row == column).astype(jnp.float32)
    row = lax.broadcasted_iota(jnp.int32, (size, BLK), 0)
    column = lax.broadcasted_iota(jnp.int32, (size, BLK), 1)

    def step(index, carry):
        base = pl.multiple_of(index * BLK, BLK)
        invert_block(work_ref[pl.ds(base, BLK), pl.ds(base, BLK)], block_ref)
        block = block_ref[...]
        below = product_3(work_ref[:, pl.ds(base, BLK)], block, transposed=True)
        right = product_3(block, work_ref[pl.ds(base, BLK), :])
        below = jnp.where(row >= column + base, below, 0.0)
        factor_ref[:, pl.ds(pl.multiple_of(first_column + base, BLK), BLK)] = below
        inverse_ref[pl.ds(base, BLK), :] = right[:, size:]
        below = jnp.where(row >= base + BLK, below, 0.0)
        work_ref[...] = work_ref[...] - product_3(below, right)
        return carry

    lax.fori_loop(0, size // BLK, step, 0)


def start_copies(plan, position_ref, source, blocks, portion, width, first, target_ref, sems):
    copies = []
    rows = plan["piece_rows"]
    members = 2 ** plan["height"]
    for order, block in enumerate(blocks):
        slot = position_ref[block % plan["front_count"]]
        for member in range(members):
            place = position_ref[plan["front_count"] + member]
            start = pl.multiple_of(order * BLK + place * rows, rows)
            copy = pltpu.make_async_copy(
                source(member, portion, block, slot).at[:, pl.ds(first, width)],
                target_ref.at[pl.ds(start, rows), pl.ds(0, width)],
                sems.at[order * members + member],
            )
            copy.start()
            copies.append(copy)
    return copies


class Child:
    def __init__(self, strips, halves, core):
        self.strips, self.halves, self.core = strips, halves, core

    def block(self, i, j):
        strip, part = i // 2, i % 2
        columns = pl.ds(j * BLK, BLK)
        if self.halves is None:
            return self.strips[strip][pl.ds(part * BLK, BLK), columns]
        mine, theirs = self.halves[strip]
        return jnp.where(self.core == part, mine[:, columns], theirs[:, columns])


def child_sum(children, i, j, weights):
    flip = i // 2 < j // 2
    total = None
    for child, weight in zip(children, weights):
        term = child.block(*((j, i) if flip else (i, j))) * weight
        total = term if total is None else total + term
    return total.T if flip else total


def make_source(plan, refs):
    if plan["height"] == 1:
        return lambda member, portion, block, slot: refs[
            (portion, block // plan["front_count"], member)
        ].at[slot]
    return lambda member, portion, block, slot: refs[member].at[
        slot, portion, block // plan["front_count"]
    ]


def unpack(plan, refs, portions, blocks, strips):
    refs = list(refs)
    position_ref, mask_ref = refs.pop(0), refs.pop(0)
    names = piece_names(plan, portions, blocks)
    pieces = {name: refs.pop(0) for name in names}
    children = []
    if plan["height"] > 1:
        own = {strip: refs.pop(0) for strip in strips}
        other = {strip: (refs.pop(0), refs.pop(0)) for strip in strips}
        core = position_ref[plan["front_count"] + 2 ** plan["height"]]
        children = [Child(own, None, core), Child(None, other, core)]
    return position_ref, mask_ref, make_source(plan, pieces), children, refs


def piece_names(plan, portions, blocks):
    members = range(2 ** plan["height"])
    if plan["height"] > 1:
        return list(members)
    slabs = sorted({block // plan["front_count"] for block in blocks})
    return [(p, t, m) for p in portions for t in slabs for m in members]


def leading(plan, state, portions, blocks, strips):
    smem = pl.BlockSpec(memory_space=pltpu.SMEM)
    anywhere = pl.BlockSpec(memory_space=pl.ANY)
    vmem = pl.BlockSpec(memory_space=pltpu.VMEM)
    operands = [state["position"], state["masks"]]
    specs = [smem, smem]
    for name in piece_names(plan, portions, blocks):
        operands.append(state["pieces"][name])
        specs.append(anywhere)
    if plan["height"] > 1:
        for strip in strips:
            operands.append(state["own"][strip])
            specs.append(vmem)
        for strip in strips:
            operands.extend(state["other"][strip])
            specs.extend([vmem, vmem])
    return operands, specs


def factor_chunk(plan, state, chunk, factors, inverses):
    low, high = plan["chunks"][chunk]
    size, width = high - low, high
    blocks = range(low // BLK, high // BLK)
    strips = range(low // STRIP, high // STRIP)
    earlier = plan["chunks"][:chunk]

    def kernel(*refs):
        position_ref, mask_ref, source, children, refs = unpack(plan, refs, (0,), blocks, strips)
        old_factors, old_inverses = refs[:chunk], refs[chunk : 2 * chunk]
        factor_ref, inverse_ref, rows_ref, work_ref, block_ref, sems = refs[2 * chunk :]
        copies = start_copies(plan, position_ref, source, blocks, 0, width, 0, rows_ref, sems)
        for copy in copies:
            copy.wait()
        if children:
            for order, i in enumerate(blocks):
                for j in range(width // BLK):
                    weights = [
                        mask_ref[c * PIVOT_BLOCKS + i] * mask_ref[c * PIVOT_BLOCKS + j] for c in (0, 1)
                    ]
                    if i // 2 < j // 2 and (i // 2) * STRIP + STRIP <= low:
                        continue
                    rows_ref[pl.ds(order * BLK, BLK), pl.ds(j * BLK, BLK)] += child_sum(
                        children, i, j, weights
                    )
        corner = rows_ref[:, pl.ds(low, size)]
        for index, (first, last) in enumerate(earlier):
            part = rows_ref[:, pl.ds(first, last - first)]
            if index:
                part = part - product_3(
                    factor_ref[:, pl.ds(0, first)], old_factors[index][:, pl.ds(0, first)], True
                )
            part = product_3(part, old_inverses[index][...], True)
            factor_ref[:, pl.ds(first, last - first)] = part
        if chunk:
            done = factor_ref[:, pl.ds(0, low)]
            corner = corner - product_3(done, done, True)
        work_ref[:, pl.ds(0, size)] = corner
        if width < plan["pivot_size"]:
            factor_ref[:, width:] = jnp.zeros((size, plan["pivot_size"] - width), jnp.float32)
        factor_in_place(work_ref, block_ref, factor_ref, low, inverse_ref)

    operands, specs = leading(plan, state, (0,), blocks, strips)
    vmem = pl.BlockSpec(memory_space=pltpu.VMEM)
    operands += factors[:chunk] + inverses[:chunk]
    specs += [vmem] * (2 * chunk)
    return pl.pallas_call(
        kernel,
        out_shape=[
            jax.ShapeDtypeStruct((size, plan["pivot_size"]), jnp.float32),
            jax.ShapeDtypeStruct((size, size), jnp.float32),
        ],
        in_specs=specs,
        out_specs=[vmem, vmem],
        scratch_shapes=[
            pltpu.VMEM((size, width), jnp.float32),
            pltpu.VMEM((size, 2 * size), jnp.float32),
            pltpu.VMEM((BLK, BLK), jnp.float32),
            pltpu.SemaphoreType.DMA((len(blocks) * 2 ** plan["height"],)),
        ],
        compiler_params=pltpu.CompilerParams(vmem_limit_bytes=48 * 2**20),
        cost_estimate=pl.CostEstimate(
            flops=60_000_000_000 * size // 1024, bytes_accessed=8 * size * width, transcendentals=0
        ),
        name=f"factor_chunk_{chunk}",
    )(*operands)


def panel_and_schur(plan, state, strips, factors, inverses, panel_before, last):
    pivot_size = plan["pivot_size"]
    blocks = range(strips[0] * STRIP // BLK, (strips[-1] + 1) * STRIP // BLK)
    size = len(blocks) * BLK
    start = strips[0] * STRIP
    chunks = plan["chunks"]
    count = len(chunks)
    everything = range(pivot_size // STRIP)
    final = strips[-1] == everything[-1]
    before = [] if panel_before is None else [panel_before]
    first_level = plan["height"] == 1
    rows = plan["piece_rows"]
    slabs = PIVOT_BLOCKS // plan["front_count"]

    def kernel(*refs):
        position_ref, mask_ref, source, children, refs = unpack(plan, refs, (1,), blocks, everything)
        factor_refs, inverse_refs = refs[:count], refs[count : 2 * count]
        refs = refs[2 * count :]
        before_refs, refs = refs[: len(before)], refs[len(before) :]
        panel_ref, refs = refs[0], refs[1:]
        if last:
            schur_refs, refs = refs[:1], refs[1:]
        else:
            schur_refs, refs = refs[: len(strips)], refs[len(strips) :]
        if final:
            own_ref, refs = refs[0], refs[1:]
        rows_ref, corner_ref, sems, corner_sems = refs
        copies = start_copies(plan, position_ref, source, blocks, 1, pivot_size, 0, rows_ref, sems)
        corner_copies = []
        if first_level:
            members = 2 ** plan["height"]
            for order, block in enumerate(blocks):
                limit = (block // plan["front_count"] + 1) * plan["front_count"] * BLK
                corner_copies += start_copies(
                    plan,
                    position_ref,
                    source,
                    [block],
                    1,
                    limit,
                    pivot_size,
                    corner_ref.at[pl.ds(order * BLK, BLK)],
                    corner_sems.at[pl.ds(order * members, members)],
                )
        for copy in copies:
            copy.wait()
        if children:
            for order, i in enumerate(blocks):
                for j in range(PIVOT_BLOCKS):
                    weights = [
                        (1.0 - mask_ref[c * PIVOT_BLOCKS + i]) * mask_ref[c * PIVOT_BLOCKS + j]
                        for c in (0, 1)
                    ]
                    rows_ref[pl.ds(order * BLK, BLK), pl.ds(j * BLK, BLK)] += child_sum(
                        children, i, j, weights
                    )
                    if last or j // 2 <= i // 2:
                        weights = [
                            (1.0 - mask_ref[c * PIVOT_BLOCKS + i])
                            * (1.0 - mask_ref[c * PIVOT_BLOCKS + j])
                            for c in (0, 1)
                        ]
                        corner_ref[pl.ds(order * BLK, BLK), pl.ds(j * BLK, BLK)] = child_sum(
                            children, i, j, weights
                        )
        for index, (low, high) in enumerate(chunks):
            part = rows_ref[:, pl.ds(low, high - low)]
            if index:
                part = part - product_3(
                    panel_ref[:, pl.ds(0, low)], factor_refs[index][:, pl.ds(0, low)], True
                )
            panel_ref[:, pl.ds(low, high - low)] = product_3(part, inverse_refs[index][...], True)
        for copy in corner_copies:
            copy.wait()
        if not last:
            for order, strip in enumerate(strips):
                mine = panel_ref[pl.ds(order * STRIP, STRIP), :]
                for column in range(strip + 1):
                    if column * STRIP < start:
                        other = before_refs[0][pl.ds(column * STRIP, STRIP), :]
                    else:
                        other = panel_ref[pl.ds(column * STRIP - start, STRIP), :]
                    schur_refs[order][:, pl.ds(column * STRIP, STRIP)] = corner_ref[
                        pl.ds(order * STRIP, STRIP), pl.ds(column * STRIP, STRIP)
                    ] - product_3(mine, other, True)
        if not final:
            return
        base = plan["front_count"] + 2 ** plan["height"] + 1
        piece = pl.multiple_of(position_ref[base + 1] * rows, rows)
        for slab in range(slabs):
            block = position_ref[base] + plan["front_count"] * slab
            line = pl.multiple_of(block * BLK + piece, rows)
            for index, (low, high) in enumerate(chunks):

                @pl.when((line >= low) & (line < high))
                def _():
                    own_ref[pl.ds(slab * rows, rows), :] = factor_refs[index][
                        pl.ds(pl.multiple_of(line - low, rows), rows), :
                    ]

            target = pl.ds((slabs + slab) * rows, rows)
            if before:

                @pl.when(line < start)
                def _():
                    own_ref[target, :] = before_refs[0][pl.ds(pl.multiple_of(line, rows), rows), :]

            @pl.when(line >= start)
            def _():
                own_ref[target, :] = panel_ref[pl.ds(pl.multiple_of(line - start, rows), rows), :]

            if last:
                schur_refs[0][pl.ds(slab * rows, rows), :] = corner_ref[pl.ds(line, rows), :]
        if last:
            mine = own_ref[pl.ds(slabs * rows, slabs * rows), :]
            schur_refs[0][...] -= product_3(mine, panel_ref[...], True)

    operands, specs = leading(plan, state, (1,), blocks, everything)
    vmem = pl.BlockSpec(memory_space=pltpu.VMEM)
    operands += factors + inverses + before
    specs += [vmem] * (2 * count + len(before))
    shapes = [(size, pivot_size)]
    if last:
        shapes.append((slabs * rows, pivot_size))
    else:
        shapes += [(STRIP, (strip + 1) * STRIP) for strip in strips]
    if final:
        shapes.append((2 * slabs * rows, pivot_size))
    copy_count = len(blocks) * 2 ** plan["height"]
    return pl.pallas_call(
        kernel,
        out_shape=[jax.ShapeDtypeStruct(shape, jnp.float32) for shape in shapes],
        in_specs=specs,
        out_specs=[vmem] * len(shapes),
        scratch_shapes=[
            pltpu.VMEM((size, pivot_size), jnp.float32),
            pltpu.VMEM((size, pivot_size), jnp.float32),
            pltpu.SemaphoreType.DMA((copy_count,)),
            pltpu.SemaphoreType.DMA((copy_count,)),
        ],
        compiler_params=pltpu.CompilerParams(vmem_limit_bytes=56 * 2**20),
        cost_estimate=pl.CostEstimate(
            flops=8_000_000_000 * size // 1024, bytes_accessed=8 * size * pivot_size, transcendentals=0
        ),
        name=f"panel_{strips[0]}",
    )(*operands)


def partner_2(value, axis, stride):
    mask = 2**stride
    pairs = [(source, source ^ mask) for source in range(lax.axis_size(axis))]
    return lax.ppermute(value, axis, pairs)


def reversed_bits(number, bit_count):
    result = jnp.zeros((), jnp.int32)
    for bit_index in range(bit_count):
        result = result + (number >> bit_index & 1) * (1 << bit_count - 1 - bit_index)
    return result


def ring_front(value):
    count = lax.axis_size("front")
    pairs = [(source, (source + 1) % count) for source in range(count)]
    slots = [value]
    for _ in range(count - 1):
        slots.append(lax.ppermute(slots[-1], "front", pairs))
    return jnp.stack(slots)


def gather_pieces(value, height):
    arrays = {0: ring_front(value)}
    for bit in reversed(range(height)):
        arrays.update({m | 1 << bit: partner_2(a, "leaf", bit) for m, a in list(arrays.items())})
    return [arrays[m] for m in range(2**height)]


def local(
    leaf_contrib,
    entries_lower,
    entries_middle,
    entries_upper,
    assembly_lower,
    assembly_middle,
    assembly_upper,
):
    front_count = lax.axis_size("front")
    slabs = PIVOT_BLOCKS // front_count
    leaf_index = lax.axis_index("leaf")
    front_index = lax.axis_index("front")
    pivot_size = leaf_contrib.shape[1]
    core = leaf_index & 1
    my_blocks = front_index + front_count * jnp.arange(slabs, dtype=jnp.int32)
    chunks = [(0, STRIP), (STRIP, 2 * STRIP), (2 * STRIP, pivot_size)]
    results = []
    schur = None
    for height, entries, routes in (
        (1, entries_lower, assembly_lower),
        (2, entries_middle, assembly_middle),
        (3, entries_upper, assembly_upper),
    ):
        piece_rows = BLK // 2**height
        plan = dict(
            height=height,
            piece_rows=piece_rows,
            front_count=front_count,
            pivot_size=pivot_size,
            chunks=chunks,
        )
        child_bit = leaf_index >> height - 1 & 1
        route_pair = lax.dynamic_index_in_dim(routes, leaf_index >> height, 0, keepdims=False)
        pivot_masks = (route_pair < PIVOT_BLOCKS).astype(jnp.float32)
        masks = jnp.where(child_bit == 0, pivot_masks, pivot_masks[::-1])
        position = jnp.concatenate(
            [
                (front_index - jnp.arange(front_count, dtype=jnp.int32)) % front_count,
                jnp.stack(
                    [
                        reversed_bits((leaf_index ^ m) & 2**height - 1, height)
                        for m in range(2**height)
                    ]
                    + [core, front_index, reversed_bits(leaf_index & 2**height - 1, height)]
                ),
            ]
        ).astype(jnp.int32)
        state = dict(position=position, masks=masks.reshape(-1))
        local_entries = entries.reshape(2, slabs, piece_rows, pivot_size)
        if height == 1:
            update = leaf_contrib.reshape(slabs, BLK, pivot_size)
            low_rows, high_rows = update[:, :piece_rows], update[:, piece_rows:]
            kept = jnp.where(child_bit == 0, low_rows, high_rows)
            outgoing = jnp.where(child_bit == 0, high_rows, low_rows)
            received = partner_2(outgoing, "leaf", 0)
            row_masks = masks[:, my_blocks]
            spread = jnp.repeat(masks, BLK, axis=1)

            def term(slab, width, row_pivot, column_pivot):
                total = 0.0
                for child, rows in enumerate((kept, received)):
                    row = row_masks[child, slab] if row_pivot else 1.0 - row_masks[child, slab]
                    column = spread[child] if column_pivot else 1.0 - spread[child]
                    total = total + rows[slab, :, :width] * (row * column[:width])[None]
                return total

            state["pieces"] = {}
            for slab in range(slabs):
                width = (slab + 1) * front_count * BLK
                value = local_entries[0, slab, :, :width] + term(slab, width, True, True)
                for m, array in enumerate(gather_pieces(value, height)):
                    state["pieces"][(0, slab, m)] = array
            for slab in range(slabs):
                width = (slab + 1) * front_count * BLK
                value = jnp.concatenate(
                    [
                        local_entries[1, slab] + term(slab, pivot_size, False, True),
                        term(slab, width, False, False),
                    ],
                    axis=1,
                )
                for m, array in enumerate(gather_pieces(value, height)):
                    state["pieces"][(1, slab, m)] = array
        else:
            state["pieces"] = dict(enumerate(gather_pieces(local_entries, height)))
            state["own"] = schur
            state["other"] = []
            for strip in schur:
                half = lax.dynamic_slice_in_dim(strip, core * BLK, BLK, 0)
                mine = partner_2(half, "leaf", height - 1)
                state["other"].append((mine, partner_2(mine, "leaf", 0)))
        factors, inverses = [], []
        for chunk in range(len(chunks)):
            factor, inverse = factor_chunk(plan, state, chunk, factors, inverses)
            factors.append(factor)
            inverses.append(inverse)
        strips = list(range(pivot_size // STRIP))
        if height < 3:
            panel, first_strip = panel_and_schur(
                plan, state, strips[:1], factors, inverses, None, False
            )
            _, *others, own = panel_and_schur(
                plan, state, strips[1:], factors, inverses, panel, False
            )
            schur = [first_strip] + others
        else:
            _, top, own = panel_and_schur(plan, state, strips, factors, inverses, None, True)
        results.append(own)
    return (results[0], results[1], results[2], top)


def solution(mesh):
    spec = P(("leaf", "front"), None)
    return jax.shard_map(
        local,
        mesh=mesh,
        in_specs=(spec, spec, spec, spec, P(), P(), P()),
        out_specs=(spec, spec, spec, spec),
        check_vma=False,
    )
```

```python
import jax
import jax.numpy as jnp
from jax import lax
from jax.experimental import pallas as pl
from jax.experimental.pallas import tpu as pltpu
from jax.sharding import PartitionSpec as P

BLK = 128
PIVOT_BLOCKS = 8
SUB = 8
STRIP = 256


def split_parts(value):
    high = value.astype(jnp.bfloat16)
    low = (value - high.astype(jnp.float32)).astype(jnp.bfloat16)
    return high, low


def product_3(left, right, transposed=False):
    dims = (((1,), (1 if transposed else 0,)), ((), ()))
    left_high, left_low = split_parts(left)
    right_high, right_low = split_parts(right)

    def one(first, second):
        return lax.dot_general(first, second, dims, preferred_element_type=jnp.float32)

    return one(left_high, right_high) + (one(left_high, right_low) + one(left_low, right_high))


def invert_block(block, inverse_ref, spare_ref):
    count = BLK // SUB
    shape = (SUB, BLK)
    rows = [block[SUB * m : SUB * m + SUB] for m in range(count)]
    lane = lax.broadcasted_iota(jnp.int32, shape, 1)
    sublane = lax.broadcasted_iota(jnp.int32, shape, 0)

    def columns(m, base):
        return [jnp.broadcast_to(rows[m][:, base + j : base + j + 1], shape) for j in range(SUB)]

    def put(slot, value):
        spare_ref[SUB * slot : SUB * slot + SUB, :] = value

    def get(slot, i):
        return spare_ref[pl.ds(SUB * slot + i, SUB, stride=0), :]

    pivot_slot, next_slot, row_slot = 0, 2 * SUB, 4 * SUB
    for j, value in enumerate(columns(0, 0)):
        put(pivot_slot + j, value)
    for k in range(count):
        base = SUB * k
        turn = k % 2 * SUB
        last = k == count - 1
        d = [[get(pivot_slot + turn + j, i) for j in range(i + 1)] for i in range(SUB)]
        inside = (lane >= base) & (lane < base + SUB)
        unit = (lane == sublane + base).astype(jnp.float32)
        put(row_slot + k % 2, jnp.where(inside, unit, rows[k]))
        y = [get(row_slot + k % 2, j) for j in range(SUB)]
        if not last:
            g = columns(k + 1, base)
            ahead = columns(k + 1, base + SUB)
        f = [[None] * SUB for _ in range(SUB)]
        inverse = [None] * SUB
        for c in range(0, SUB, 2):
            e = c + 1
            p, q, r = d[c][c], d[e][c], d[e][e]
            inverse[c] = 1.0 / p
            both = 1.0 / (p * r - q * q)
            inverse[e] = p * both
            f[e][c] = q * inverse[c]
            h = {}
            for i in range(e + 1, SUB):
                f[i][c] = d[i][c] * inverse[c]
                h[i] = p * d[i][e] - q * d[i][c]
                f[i][e] = h[i] * both
            for i in range(e + 1, SUB):
                w = r * d[i][c] - q * d[i][e]
                for j in range(e + 1, i + 1):
                    d[i][j] = d[i][j] - (w * d[j][c] + h[i] * d[j][e]) * both
            for x in (c, e):
                if not last:
                    put(next_slot + turn + x, g[x])
                    scaled = g[x] * inverse[x]
                    for j in range(SUB):
                        ahead[j] = ahead[j] - scaled * get(next_slot + turn + x, j)
                for i in range(x + 1, SUB):
                    if not last:
                        g[i] = g[i] - f[i][x] * g[x]
                    y[i] = y[i] - f[i][x] * y[x]
        keep = lane[0:1] < base + SUB
        for c in range(SUB):
            row = (lax.rsqrt(inverse[c]) * inverse[c] * y[c])[0:1]
            inverse_ref[base + c : base + c + 1, :] = jnp.where(keep, row, 0.0)
        if last:
            break
        for j in range(SUB):
            put(pivot_slot + SUB - turn + j, ahead[j])
        if k + 2 < count:
            z = [a * b for a, b in zip(y, inverse)]
            for i in reversed(range(SUB)):
                for c in range(i):
                    z[c] = z[c] - f[i][c] * z[i]
        for m in range(k + 1, count):
            cleared = jnp.where(inside, 0.0, rows[m])
            if m == k + 1:
                for c in range(SUB):
                    cleared = cleared - (g[c] * y[c]) * inverse[c]
            else:
                terms = [a * b for a, b in zip(columns(m, base), z)]
                while len(terms) > 1:
                    terms = [a + b for a, b in zip(terms[::2], terms[1::2])]
                cleared = cleared - terms[0]
            rows[m] = cleared


def factor_in_place(work_ref, block_ref, spare_ref, factor_ref, first_column, inverse_ref):
    size = work_ref.shape[0]
    steps = size // BLK
    row = lax.broadcasted_iota(jnp.int32, (BLK, BLK), 0)
    column = lax.broadcasted_iota(jnp.int32, (BLK, BLK), 1)

    def step(index, carry):
        base = pl.multiple_of(index * BLK, BLK)
        invert_block(work_ref[pl.ds(base, BLK), pl.ds(base, BLK)], block_ref, spare_ref)
        for now in range(steps):

            @pl.when(index == now)
            def _():
                low, high = now * BLK, now * BLK + BLK
                block = block_ref[...]
                below = product_3(work_ref[low:, low:high], block, True)
                if now:
                    factor_ref[0:low, first_column + low : first_column + high] = jnp.zeros(
                        (low, BLK), jnp.float32
                    )
                factor_ref[low:high, first_column + low : first_column + high] = jnp.where(
                    row >= column, below[:BLK], 0.0
                )
                inverse_ref[low:high, low:high] = block
                if high < size:
                    inverse_ref[low:high, high:] = jnp.zeros((BLK, size - high), jnp.float32)
                    below = below[BLK:]
                    factor_ref[high:, first_column + low : first_column + high] = below
                    right = product_3(block, work_ref[low:high, high:])
                    work_ref[high:, high:] = work_ref[high:, high:] - product_3(below, right)
                    work_ref[high:, low:high] = -product_3(below, block)
                if now:
                    left = product_3(block, work_ref[low:high, :low])
                    inverse_ref[low:high, :low] = left
                    if high < size:
                        work_ref[high:, :low] = work_ref[high:, :low] - product_3(below, left)

        return carry

    lax.fori_loop(0, steps, step, 0)


def start_copies(plan, position_ref, source, blocks, portion, width, first, target_ref, sems):
    copies = []
    rows = plan["piece_rows"]
    members = 2 ** plan["height"]
    for order, block in enumerate(blocks):
        slot = block % plan["front_count"]
        if plan["where"][(portion, block // plan["front_count"])][0] in plan["direct"]:
            slot = position_ref[slot]
        for member in range(members):
            place = position_ref[plan["front_count"] + member]
            start = pl.multiple_of(order * BLK + place * rows, rows)
            copy = pltpu.make_async_copy(
                source(member, portion, block, slot).at[:, pl.ds(first, width)],
                target_ref.at[pl.ds(start, rows), pl.ds(0, width)],
                sems.at[order * members + member],
            )
            copy.start()
            copies.append(copy)
    return copies


class Child:
    def __init__(self, strips, halves, core):
        self.strips, self.halves, self.core = strips, halves, core

    def block(self, i, j):
        strip, part = i // 2, i % 2
        columns = pl.ds(j * BLK, BLK)
        if self.halves is None:
            return self.strips[strip][pl.ds(part * BLK, BLK), columns]
        mine, theirs = self.halves[strip]
        return jnp.where(self.core == part, mine[:, columns], theirs[:, columns])


def child_sum(children, i, j, weights):
    flip = i // 2 < j // 2
    total = None
    for child, weight in zip(children, weights):
        term = child.block(*((j, i) if flip else (i, j))) * weight
        total = term if total is None else total + term
    return total.T if flip else total


def stack_index(member, height):
    return sum((member >> bit & 1) << height - 1 - bit for bit in range(1, height))


def make_source(plan, refs):
    height = plan["height"]

    def source(member, portion, block, slot):
        group, index = plan["where"][(portion, block // plan["front_count"])]
        ref = refs[(group, member & 1)].at[stack_index(member, height), slot]
        return ref if index is None else ref.at[index]

    return source


def unpack(plan, refs, portions, blocks, strips):
    refs = list(refs)
    position_ref, mask_ref = refs.pop(0), refs.pop(0)
    names = piece_names(plan, portions, blocks)
    pieces = {name: refs.pop(0) for name in names}
    children = []
    if plan["height"] > 1:
        own = {strip: refs.pop(0) for strip in strips}
        other = {strip: (refs.pop(0), refs.pop(0)) for strip in strips}
        core = position_ref[plan["front_count"] + 2 ** plan["height"]]
        children = [Child(own, None, core), Child(None, other, core)]
    return position_ref, mask_ref, make_source(plan, pieces), children, refs


def piece_names(plan, portions, blocks):
    slabs = sorted({block // plan["front_count"] for block in blocks})
    groups = sorted({plan["where"][(p, t)][0] for p in portions for t in slabs})
    return [(group, c) for group in groups for c in (0, 1)]


def leading(plan, state, portions, blocks, strips):
    smem = pl.BlockSpec(memory_space=pltpu.SMEM)
    anywhere = pl.BlockSpec(memory_space=pl.ANY)
    vmem = pl.BlockSpec(memory_space=pltpu.VMEM)
    operands = [state["position"], state["masks"]]
    specs = [smem, smem]
    for name in piece_names(plan, portions, blocks):
        operands.append(state["pieces"][name])
        specs.append(anywhere)
    if plan["height"] > 1:
        for strip in strips:
            operands.append(state["own"][strip])
            specs.append(vmem)
        for strip in strips:
            operands.extend(state["other"][strip])
            specs.extend([vmem, vmem])
    return operands, specs


def factor_chunk(plan, state, chunk, factors, inverses):
    low, high = plan["chunks"][chunk]
    size, width = high - low, high
    blocks = range(low // BLK, high // BLK)
    strips = range(low // STRIP, high // STRIP)
    earlier = plan["chunks"][:chunk]

    def kernel(*refs):
        position_ref, mask_ref, source, children, refs = unpack(plan, refs, (0,), blocks, strips)
        old_factors, old_inverses = refs[:chunk], refs[chunk : 2 * chunk]
        factor_ref, inverse_ref, rows_ref, work_ref, block_ref, spare_ref, sems = refs[2 * chunk :]
        copies = start_copies(plan, position_ref, source, blocks, 0, width, 0, rows_ref, sems)
        for copy in copies:
            copy.wait()
        if children:
            for order, i in enumerate(blocks):
                for j in range(width // BLK):
                    weights = [
                        mask_ref[c * PIVOT_BLOCKS + i] * mask_ref[c * PIVOT_BLOCKS + j] for c in (0, 1)
                    ]
                    rows_ref[pl.ds(order * BLK, BLK), pl.ds(j * BLK, BLK)] += child_sum(
                        children, i, j, weights
                    )
        corner = rows_ref[:, pl.ds(low, size)]
        for index, (first, last) in enumerate(earlier):
            part = rows_ref[:, pl.ds(first, last - first)]
            if index:
                part = part - product_3(
                    factor_ref[:, pl.ds(0, first)], old_factors[index][:, pl.ds(0, first)], True
                )
            part = product_3(part, old_inverses[index][...], True)
            factor_ref[:, pl.ds(first, last - first)] = part
        if chunk:
            done = factor_ref[:, pl.ds(0, low)]
            corner = corner - product_3(done, done, True)
        work_ref[...] = corner
        if width < plan["pivot_size"]:
            factor_ref[:, width:] = jnp.zeros((size, plan["pivot_size"] - width), jnp.float32)
        factor_in_place(work_ref, block_ref, spare_ref, factor_ref, low, inverse_ref)

    operands, specs = leading(plan, state, (0,), blocks, strips)
    vmem = pl.BlockSpec(memory_space=pltpu.VMEM)
    operands += factors[:chunk] + inverses[:chunk]
    specs += [vmem] * (2 * chunk)
    return pl.pallas_call(
        kernel,
        out_shape=[
            jax.ShapeDtypeStruct((size, plan["pivot_size"]), jnp.float32),
            jax.ShapeDtypeStruct((size, size), jnp.float32),
        ],
        in_specs=specs,
        out_specs=[vmem, vmem],
        scratch_shapes=[
            pltpu.VMEM((size, width), jnp.float32),
            pltpu.VMEM((size, size), jnp.float32),
            pltpu.VMEM((BLK, BLK), jnp.float32),
            pltpu.VMEM((SUB * (4 * SUB + 2), BLK), jnp.float32),
            pltpu.SemaphoreType.DMA((len(blocks) * 2 ** plan["height"],)),
        ],
        compiler_params=pltpu.CompilerParams(vmem_limit_bytes=48 * 2**20),
        cost_estimate=pl.CostEstimate(
            flops=60_000_000_000 * size // 1024, bytes_accessed=8 * size * width, transcendentals=0
        ),
        name=f"factor_chunk_{chunk}",
    )(*operands)


def panel_and_schur(plan, state, strips, factors, inverses, panel_before, last):
    pivot_size = plan["pivot_size"]
    blocks = range(strips[0] * STRIP // BLK, (strips[-1] + 1) * STRIP // BLK)
    size = len(blocks) * BLK
    start = strips[0] * STRIP
    chunks = plan["chunks"]
    count = len(chunks)
    everything = range(pivot_size // STRIP)
    final = strips[-1] == everything[-1]
    before = [] if panel_before is None else [panel_before]
    first_level = plan["height"] == 1
    rows = plan["piece_rows"]
    slabs = PIVOT_BLOCKS // plan["front_count"]

    def kernel(*refs):
        position_ref, mask_ref, source, children, refs = unpack(plan, refs, (1,), blocks, everything)
        factor_refs, inverse_refs = refs[:count], refs[count : 2 * count]
        refs = refs[2 * count :]
        before_refs, refs = refs[: len(before)], refs[len(before) :]
        panel_ref, refs = refs[0], refs[1:]
        if last:
            schur_refs, refs = refs[:1], refs[1:]
        else:
            schur_refs, refs = refs[: len(strips)], refs[len(strips) :]
        if final:
            own_ref, refs = refs[0], refs[1:]
        rows_ref, corner_ref, sems, corner_sems = refs
        copies = start_copies(plan, position_ref, source, blocks, 1, pivot_size, 0, rows_ref, sems)
        corner_copies = []
        if first_level:
            members = 2 ** plan["height"]
            for order, block in enumerate(blocks):
                limit = (block // plan["front_count"] + 1) * plan["front_count"] * BLK
                corner_copies += start_copies(
                    plan,
                    position_ref,
                    source,
                    [block],
                    1,
                    limit,
                    pivot_size,
                    corner_ref.at[pl.ds(order * BLK, BLK)],
                    corner_sems.at[pl.ds(order * members, members)],
                )
        for copy in copies:
            copy.wait()
        if children:
            for order, i in enumerate(blocks):
                for j in range(PIVOT_BLOCKS):
                    weights = [
                        (1.0 - mask_ref[c * PIVOT_BLOCKS + i]) * mask_ref[c * PIVOT_BLOCKS + j]
                        for c in (0, 1)
                    ]
                    rows_ref[pl.ds(order * BLK, BLK), pl.ds(j * BLK, BLK)] += child_sum(
                        children, i, j, weights
                    )
                    if last or j // 2 <= i // 2:
                        weights = [
                            (1.0 - mask_ref[c * PIVOT_BLOCKS + i])
                            * (1.0 - mask_ref[c * PIVOT_BLOCKS + j])
                            for c in (0, 1)
                        ]
                        corner_ref[pl.ds(order * BLK, BLK), pl.ds(j * BLK, BLK)] = child_sum(
                            children, i, j, weights
                        )
        for index, (low, high) in enumerate(chunks):
            part = rows_ref[:, pl.ds(low, high - low)]
            if index:
                part = part - product_3(
                    panel_ref[:, pl.ds(0, low)], factor_refs[index][:, pl.ds(0, low)], True
                )
            panel_ref[:, pl.ds(low, high - low)] = product_3(part, inverse_refs[index][...], True)
        for copy in corner_copies:
            copy.wait()
        if not last:
            for order, strip in enumerate(strips):
                mine = panel_ref[pl.ds(order * STRIP, STRIP), :]
                for column in range(strip + 1):
                    if column * STRIP < start:
                        other = before_refs[0][pl.ds(column * STRIP, STRIP), :]
                    else:
                        other = panel_ref[pl.ds(column * STRIP - start, STRIP), :]
                    schur_refs[order][:, pl.ds(column * STRIP, STRIP)] = corner_ref[
                        pl.ds(order * STRIP, STRIP), pl.ds(column * STRIP, STRIP)
                    ] - product_3(mine, other, True)
        if not final:
            return
        base = plan["front_count"] + 2 ** plan["height"] + 1
        piece = pl.multiple_of(position_ref[base + 1] * rows, rows)
        for slab in range(slabs):
            block = position_ref[base] + plan["front_count"] * slab
            line = pl.multiple_of(block * BLK + piece, rows)
            for index, (low, high) in enumerate(chunks):

                @pl.when((line >= low) & (line < high))
                def _():
                    own_ref[pl.ds(slab * rows, rows), :] = factor_refs[index][
                        pl.ds(pl.multiple_of(line - low, rows), rows), :
                    ]

            target = pl.ds((slabs + slab) * rows, rows)
            if before:

                @pl.when(line < start)
                def _():
                    own_ref[target, :] = before_refs[0][pl.ds(pl.multiple_of(line, rows), rows), :]

            @pl.when(line >= start)
            def _():
                own_ref[target, :] = panel_ref[pl.ds(pl.multiple_of(line - start, rows), rows), :]

            if last:
                schur_refs[0][pl.ds(slab * rows, rows), :] = corner_ref[pl.ds(line, rows), :]
        if last:
            mine = own_ref[pl.ds(slabs * rows, slabs * rows), :]
            schur_refs[0][...] -= product_3(mine, panel_ref[...], True)

    operands, specs = leading(plan, state, (1,), blocks, everything)
    vmem = pl.BlockSpec(memory_space=pltpu.VMEM)
    operands += factors + inverses + before
    specs += [vmem] * (2 * count + len(before))
    shapes = [(size, pivot_size)]
    if last:
        shapes.append((slabs * rows, pivot_size))
    else:
        shapes += [(STRIP, (strip + 1) * STRIP) for strip in strips]
    if final:
        shapes.append((2 * slabs * rows, pivot_size))
    copy_count = len(blocks) * 2 ** plan["height"]
    return pl.pallas_call(
        kernel,
        out_shape=[jax.ShapeDtypeStruct(shape, jnp.float32) for shape in shapes],
        in_specs=specs,
        out_specs=[vmem] * len(shapes),
        scratch_shapes=[
            pltpu.VMEM((size, pivot_size), jnp.float32),
            pltpu.VMEM((size, pivot_size), jnp.float32),
            pltpu.SemaphoreType.DMA((copy_count,)),
            pltpu.SemaphoreType.DMA((copy_count,)),
        ],
        compiler_params=pltpu.CompilerParams(vmem_limit_bytes=56 * 2**20),
        cost_estimate=pl.CostEstimate(
            flops=20_000_000_000 * size // 1024, bytes_accessed=8 * size * pivot_size, transcendentals=0
        ),
        name=f"panel_{strips[0]}",
    )(*operands)


def partner_2(value, axis, stride):
    mask = 2**stride
    pairs = [(source, source ^ mask) for source in range(lax.axis_size(axis))]
    return lax.ppermute(value, axis, pairs)


def reversed_bits(number, bit_count):
    result = jnp.zeros((), jnp.int32)
    for bit_index in range(bit_count):
        result = result + (number >> bit_index & 1) * (1 << bit_count - 1 - bit_index)
    return result


def all_front(value):
    count = lax.axis_size("front")
    slots = [value]
    for mask in range(1, count):
        pairs = [(source, source ^ mask) for source in range(count)]
        slots.append(lax.ppermute(value, "front", pairs))
    return jnp.stack(slots)


def after(value, done):
    corner = done.reshape(-1)[:1]
    return value + jnp.where(corner > jnp.inf, 1.0, 0.0).reshape((1,) * value.ndim)


def local(
    leaf_contrib,
    entries_lower,
    entries_middle,
    entries_upper,
    assembly_lower,
    assembly_middle,
    assembly_upper,
):
    front_count = lax.axis_size("front")
    slabs = PIVOT_BLOCKS // front_count
    leaf_index = lax.axis_index("leaf")
    front_index = lax.axis_index("front")
    pivot_size = leaf_contrib.shape[1]
    core = leaf_index & 1
    my_blocks = front_index + front_count * jnp.arange(slabs, dtype=jnp.int32)
    chunks = [(0, STRIP), (STRIP, 2 * STRIP), (2 * STRIP, pivot_size)]
    plans, states, entry_slabs = {}, {}, {}
    names = [(p, t) for p in (0, 1) for t in range(slabs)]
    where = {
        1: {name: (order, None) for order, name in enumerate(names)},
        2: {(p, t): (slabs, t) if p else (t, None) for p, t in names},
        3: {(p, t): (p * slabs + t, None) for p, t in names},
    }
    direct = {1: (0,), 2: range(slabs), 3: range(2 * slabs)}
    for height, entries, routes in (
        (1, entries_lower, assembly_lower),
        (2, entries_middle, assembly_middle),
        (3, entries_upper, assembly_upper),
    ):
        piece_rows = BLK // 2**height
        plans[height] = dict(
            height=height,
            piece_rows=piece_rows,
            front_count=front_count,
            pivot_size=pivot_size,
            chunks=chunks,
            where=where[height],
            direct=direct[height],
        )
        child_bit = leaf_index >> height - 1 & 1
        route_pair = lax.dynamic_index_in_dim(routes, leaf_index >> height, 0, keepdims=False)
        pivot_masks = (route_pair < PIVOT_BLOCKS).astype(jnp.float32)
        masks = jnp.where(child_bit == 0, pivot_masks, pivot_masks[::-1])
        position = jnp.concatenate(
            [
                front_index ^ jnp.arange(front_count, dtype=jnp.int32),
                jnp.stack(
                    [
                        reversed_bits((leaf_index ^ m) & 2**height - 1, height)
                        for m in range(2**height)
                    ]
                    + [core, front_index, reversed_bits(leaf_index & 2**height - 1, height)]
                ),
            ]
        ).astype(jnp.int32)
        states[height] = dict(position=position, masks=masks.reshape(-1), pieces={})
        entry_slabs[height] = entries.reshape(2, slabs, piece_rows, pivot_size)

    piece_rows = BLK // 2
    update = leaf_contrib.reshape(slabs, BLK, pivot_size)
    low_rows, high_rows = update[:, :piece_rows], update[:, piece_rows:]
    kept = jnp.where(core == 0, low_rows, high_rows)
    received = partner_2(jnp.where(core == 0, high_rows, low_rows), "leaf", 0)
    masks = states[1]["masks"].reshape(2, PIVOT_BLOCKS)
    row_masks = masks[:, my_blocks]
    spread = jnp.repeat(masks, BLK, axis=1)

    def term(slab, width, row_pivot, column_pivot):
        total = 0.0
        for child, rows in enumerate((kept, received)):
            row = row_masks[child, slab] if row_pivot else 1.0 - row_masks[child, slab]
            column = spread[child] if column_pivot else 1.0 - spread[child]
            total = total + rows[slab, :, :width] * (row * column[:width])[None]
        return total

    def slab_width(slab):
        return (slab + 1) * front_count * BLK

    lower_values = {}
    for slab in range(slabs):
        width = slab_width(slab)
        lower_values[(0, slab)] = entry_slabs[1][0, slab, :, :width] + term(slab, width, True, True)
        lower_values[(1, slab)] = jnp.concatenate(
            [
                entry_slabs[1][1, slab] + term(slab, pivot_size, False, True),
                term(slab, width, False, False),
            ],
            axis=1,
        )

    for height in (2, 3):
        states[height]["own"], states[height]["other"] = {}, {}
    factors = {1: [], 2: [], 3: []}
    inverses = {1: [], 2: [], 3: []}
    now = [leaf_contrib]

    def ready(value):
        return lax.optimization_barrier((value, now[0]))[0]

    def end_step(*results):
        now[0] = results

    def gather(value):
        return lax.all_gather(ready(value), "front")

    def across(value, bit):
        value = ready(value)
        return value, partner_2(value, "leaf", bit)

    def joined(pair):
        return jnp.concatenate(pair, axis=0)

    def place(height, group, stack):
        stack = ready(stack)
        pieces = (stack, partner_2(stack, "leaf", 0))
        for index, piece in enumerate(pieces):
            states[height]["pieces"][(group, index)] = piece
        return pieces[1]

    def offer(height, strip):
        half = lax.dynamic_slice_in_dim(states[height]["own"][strip], core * BLK, BLK, 0)
        return partner_2(ready(half), "leaf", height - 1)

    def swap(height, strip, mine):
        theirs = partner_2(ready(mine), "leaf", 0)
        states[height]["other"][strip] = (mine, theirs)
        return theirs

    def factor(height, chunk):
        states[height]["position"] = ready(states[height]["position"])
        one, other = factor_chunk(
            plans[height], states[height], chunk, factors[height], inverses[height]
        )
        factors[height].append(one)
        inverses[height].append(other)
        return other

    def panel(height, strips, before, last=False):
        states[height]["position"] = ready(states[height]["position"])
        outputs = panel_and_schur(
            plans[height], states[height], strips, factors[height], inverses[height], before, last
        )
        if not last:
            for strip, value in zip(strips, outputs[1:]):
                states[height + 1]["own"][strip] = value
        return outputs

    strips = list(range(pivot_size // STRIP))
    later = range(1, slabs)
    middle = all_front(entry_slabs[2][0, 0, :, : slab_width(0)])[None]
    first = all_front(lower_values[(0, 0)])
    end_step(middle, first)
    end_step(place(1, 0, first[None]))

    pair = across(middle, 1)
    pivots = [gather(after(lower_values[(0, t)], first)) for t in later]
    end_step(factor(1, 0), pair)

    taken = place(2, 0, joined(pair))
    updates = [gather(lower_values[(1, 0)])]
    end_step(factor(1, 1), taken)

    end_step(*[place(1, t, ready(value)[None]) for t, value in zip(later, pivots)])

    updates += [gather(lower_values[(1, t)]) for t in later]
    end_step(factor(1, 2))

    middle_update = gather(entry_slabs[2][1])
    end_step(place(1, slabs, ready(updates[0])[None]))

    panel_0, _ = panel(1, [0], None)
    end_step(panel_0)

    mine_0 = offer(2, 0)
    panel_1, _ = panel(1, [1], panel_0)
    end_step(panel_1, mine_0)

    end_step(swap(2, 0, mine_0))

    mine_1 = offer(2, 1)
    middle = [all_front(ready(entry_slabs[2][0, t]))[None] for t in later]
    end_step(factor(2, 0), mine_1, middle)

    taken = swap(2, 1, mine_1)
    end_step(taken)

    pairs = [across(value, 1) for value in middle]
    taken = [place(1, slabs + t, ready(updates[t])[None]) for t in later]
    end_step(factor(2, 1), pairs, taken)

    taken = [place(2, t, joined(pair)) for t, pair in zip(later, pairs)]
    upper = [all_front(ready(entry_slabs[3][0, t]))[None] for t in range(slabs)]
    before = jnp.concatenate([panel_0, panel_1], axis=0)
    panel_2, _ = panel(1, [2], before)
    end_step(panel_2, taken, upper)

    mine_2 = offer(2, 2)
    upper_update = [all_front(ready(entry_slabs[3][1, t]))[None] for t in range(slabs)]
    before = jnp.concatenate([before, panel_2], axis=0)
    panel_3, _, lower_own = panel(1, [3], before)
    end_step(panel_3, mine_2, upper_update)

    mine_3 = offer(2, 3)
    taken = swap(2, 2, mine_2)
    end_step(mine_3, taken)
    end_step(swap(2, 3, mine_3))

    pair = across(middle_update[None], 1)
    pairs = [across(value, 2) for value in upper + upper_update]
    end_step(factor(2, 2), pair, pairs)

    taken = place(2, slabs, joined(pair))
    upper = [joined(pair) for pair in pairs]
    end_step(taken, upper)

    panel_0, _ = panel(2, [0], None)
    end_step(panel_0)

    mine_0 = offer(3, 0)
    panel_1, _ = panel(2, [1], panel_0)
    end_step(panel_1, mine_0)

    mine_1 = offer(3, 1)
    taken = swap(3, 0, mine_0)
    pair = across(upper[0], 1)
    before = jnp.concatenate([panel_0, panel_1], axis=0)
    _, _, _, middle_own = panel(2, [2, 3], before)
    end_step(middle_own, mine_1, taken, pair)

    taken = place(3, 0, joined(pair)), swap(3, 1, mine_1)
    end_step(taken)

    mine_2, mine_3 = offer(3, 2), offer(3, 3)
    pairs = [across(upper[t], 1) for t in later]
    end_step(factor(3, 0), mine_2, mine_3, pairs)

    taken = swap(3, 2, mine_2), swap(3, 3, mine_3)
    taken += tuple(place(3, t, joined(pair)) for t, pair in zip(later, pairs))
    pair = across(upper[slabs], 1)
    end_step(factor(3, 1), taken, pair)

    taken = place(3, slabs, joined(pair))
    pairs = [across(upper[slabs + t], 1) for t in later]
    end_step(factor(3, 2), taken, pairs)

    end_step(*[place(3, slabs + t, joined(pair)) for t, pair in zip(later, pairs)])
    _, top, upper_own = panel(3, strips, None, True)
    return (lower_own, middle_own, upper_own, top)


def solution(mesh):
    spec = P(("leaf", "front"), None)
    return jax.shard_map(
        local,
        mesh=mesh,
        in_specs=(spec, spec, spec, spec, P(), P(), P()),
        out_specs=(spec, spec, spec, spec),
        check_vma=False,
    )
```

```python
import jax
import jax.numpy as jnp
from jax import lax
from jax.experimental import pallas as pl
from jax.experimental.pallas import tpu as pltpu
from jax.sharding import PartitionSpec as P

BLK = 128
PIVOT_BLOCKS = 8
SUB = 8
STRIP = 256


def split_parts(value):
    high = value.astype(jnp.bfloat16)
    low = (value - high.astype(jnp.float32)).astype(jnp.bfloat16)
    return high, low


def product_3(left, right, transposed=False):
    dims = (((1,), (1 if transposed else 0,)), ((), ()))
    left_high, left_low = split_parts(left)
    right_high, right_low = split_parts(right)

    def one(first, second):
        return lax.dot_general(first, second, dims, preferred_element_type=jnp.float32)

    return one(left_high, right_high) + (one(left_high, right_low) + one(left_low, right_high))


def invert_block(block, inverse_ref, spare_ref):
    count = BLK // SUB
    shape = (SUB, BLK)
    rows = [block[SUB * m : SUB * m + SUB] for m in range(count)]
    lane = lax.broadcasted_iota(jnp.int32, shape, 1)
    sublane = lax.broadcasted_iota(jnp.int32, shape, 0)

    def columns(m, base):
        return [jnp.broadcast_to(rows[m][:, base + j : base + j + 1], shape) for j in range(SUB)]

    def put(slot, value):
        spare_ref[SUB * slot : SUB * slot + SUB, :] = value

    def get(slot, i):
        return spare_ref[pl.ds(SUB * slot + i, SUB, stride=0), :]

    pivot_slot, next_slot, row_slot = 0, 2 * SUB, 4 * SUB
    for j, value in enumerate(columns(0, 0)):
        put(pivot_slot + j, value)
    for k in range(count):
        base = SUB * k
        turn = k % 2 * SUB
        last = k == count - 1
        d = [[get(pivot_slot + turn + j, i) for j in range(i + 1)] for i in range(SUB)]
        inside = (lane >= base) & (lane < base + SUB)
        unit = (lane == sublane + base).astype(jnp.float32)
        put(row_slot + k % 2, jnp.where(inside, unit, rows[k]))
        y = [get(row_slot + k % 2, j) for j in range(SUB)]
        if not last:
            g = columns(k + 1, base)
            ahead = columns(k + 1, base + SUB)
        f = [[None] * SUB for _ in range(SUB)]
        inverse = [None] * SUB
        for c in range(0, SUB, 2):
            e = c + 1
            p, q, r = d[c][c], d[e][c], d[e][e]
            inverse[c] = 1.0 / p
            both = 1.0 / (p * r - q * q)
            inverse[e] = p * both
            f[e][c] = q * inverse[c]
            h = {}
            for i in range(e + 1, SUB):
                f[i][c] = d[i][c] * inverse[c]
                h[i] = p * d[i][e] - q * d[i][c]
                f[i][e] = h[i] * both
            for i in range(e + 1, SUB):
                w = r * d[i][c] - q * d[i][e]
                for j in range(e + 1, i + 1):
                    d[i][j] = d[i][j] - (w * d[j][c] + h[i] * d[j][e]) * both
            for x in (c, e):
                if not last:
                    put(next_slot + turn + x, g[x])
                    scaled = g[x] * inverse[x]
                    for j in range(SUB):
                        ahead[j] = ahead[j] - scaled * get(next_slot + turn + x, j)
                for i in range(x + 1, SUB):
                    if not last:
                        g[i] = g[i] - f[i][x] * g[x]
                    y[i] = y[i] - f[i][x] * y[x]
        keep = lane[0:1] < base + SUB
        for c in range(SUB):
            row = (lax.rsqrt(inverse[c]) * inverse[c] * y[c])[0:1]
            inverse_ref[base + c : base + c + 1, :] = jnp.where(keep, row, 0.0)
        if last:
            break
        for j in range(SUB):
            put(pivot_slot + SUB - turn + j, ahead[j])
        if k + 2 < count:
            z = [a * b for a, b in zip(y, inverse)]
            for i in reversed(range(SUB)):
                for c in range(i):
                    z[c] = z[c] - f[i][c] * z[i]
        for m in range(k + 1, count):
            cleared = jnp.where(inside, 0.0, rows[m])
            if m == k + 1:
                for c in range(SUB):
                    cleared = cleared - (g[c] * y[c]) * inverse[c]
            else:
                terms = [a * b for a, b in zip(columns(m, base), z)]
                while len(terms) > 1:
                    terms = [a + b for a, b in zip(terms[::2], terms[1::2])]
                cleared = cleared - terms[0]
            rows[m] = cleared


def factor_in_place(work_ref, block_ref, spare_ref, factor_ref, first_column, inverse_ref):
    size = work_ref.shape[0]
    steps = size // BLK
    row = lax.broadcasted_iota(jnp.int32, (BLK, BLK), 0)
    column = lax.broadcasted_iota(jnp.int32, (BLK, BLK), 1)

    def step(index, carry):
        base = pl.multiple_of(index * BLK, BLK)
        invert_block(work_ref[pl.ds(base, BLK), pl.ds(base, BLK)], block_ref, spare_ref)
        for now in range(steps):

            @pl.when(index == now)
            def _():
                low, high = now * BLK, now * BLK + BLK
                block = block_ref[...]
                below = product_3(work_ref[low:, low:high], block, True)
                if now:
                    factor_ref[0:low, first_column + low : first_column + high] = jnp.zeros(
                        (low, BLK), jnp.float32
                    )
                factor_ref[low:high, first_column + low : first_column + high] = jnp.where(
                    row >= column, below[:BLK], 0.0
                )
                inverse_ref[low:high, low:high] = block
                if high < size:
                    inverse_ref[low:high, high:] = jnp.zeros((BLK, size - high), jnp.float32)
                    below = below[BLK:]
                    factor_ref[high:, first_column + low : first_column + high] = below
                    right = product_3(block, work_ref[low:high, high:])
                    work_ref[high:, high:] = work_ref[high:, high:] - product_3(below, right)
                    work_ref[high:, low:high] = -product_3(below, block)
                if now:
                    left = product_3(block, work_ref[low:high, :low])
                    inverse_ref[low:high, :low] = left
                    if high < size:
                        work_ref[high:, :low] = work_ref[high:, :low] - product_3(below, left)

        return carry

    lax.fori_loop(0, steps, step, 0)


class Here:
    def __init__(self, plan, routes_ref):
        height = plan["height"]
        leaf = lax.axis_index("leaf")
        self.front = lax.axis_index("front")
        self.core = leaf & 1
        self.members = leaf & 2**height - 1
        self.height = height
        self.parent = leaf >> height
        self.child = leaf >> height - 1 & 1
        self.routes_ref = routes_ref

    def piece(self, member):
        return reversed_bits(self.members ^ member, self.height)

    def to_pivot(self, child, block):
        route = self.routes_ref[self.parent, self.child ^ child, block]
        return jnp.where(route < PIVOT_BLOCKS, 1.0, 0.0)


def reversed_bits(number, bit_count):
    result = 0
    for bit_index in range(bit_count):
        result = result + (number >> bit_index & 1) * (1 << bit_count - 1 - bit_index)
    return result


def start_copies(plan, here, source, blocks, portion, width, first, target_ref, sems):
    copies = []
    rows = plan["piece_rows"]
    members = 2 ** plan["height"]
    count = plan["front_count"]
    blocks = list(blocks)
    for slab in sorted({block // count for block in blocks}):
        fronts = [block % count for block in blocks if block // count == slab]
        order = blocks.index(slab * count + fronts[0])
        group, index = plan["where"][(portion, slab)]
        for member in range(members):
            start = pl.multiple_of(here.piece(member) * rows, rows)
            ref = source(group, member)
            if group in plan["direct"]:
                spans = [(front, 1, here.front ^ front) for front in fronts]
            else:
                spans = [(fronts[0], len(fronts), fronts[0])]
            for front, length, slot in spans:
                at = order + front - fronts[0]
                slots = ref.at[pl.ds(slot, length)]
                if index is not None:
                    slots = slots.at[:, index]
                copy = pltpu.make_async_copy(
                    slots.at[:, :, pl.ds(first, width)],
                    target_ref.at[pl.ds(at, length), pl.ds(start, rows), pl.ds(0, width)],
                    sems.at[at * members + member],
                )
                copy.start()
                copies.append(copy)
    return copies


class Child:
    def __init__(self, strips, halves, core):
        self.strips, self.halves, self.core = strips, halves, core

    def block(self, i, j):
        strip, part = i // 2, i % 2
        columns = pl.ds(j * BLK, BLK)
        if self.halves is None:
            return self.strips[strip][pl.ds(part * BLK, BLK), columns]
        mine, theirs = self.halves[strip]
        return jnp.where(self.core == part, mine[:, columns], theirs[:, columns])


def child_sum(children, i, j, weights):
    flip = i // 2 < j // 2
    total = None
    for child, weight in zip(children, weights):
        term = child.block(*((j, i) if flip else (i, j))) * weight
        total = term if total is None else total + term
    return total.T if flip else total


def stack_index(member, height):
    return sum((member >> bit & 1) << height - 1 - bit for bit in range(1, height))


def make_source(plan, refs):
    height = plan["height"]

    def source(group, member):
        return refs[(group, member & 1)].at[stack_index(member, height)]

    return source


def unpack(plan, refs, portions, blocks, strips):
    refs = list(refs)
    here = Here(plan, refs.pop(0))
    names = piece_names(plan, portions, blocks)
    pieces = {name: refs.pop(0) for name in names}
    children = []
    if plan["height"] > 1:
        own = {strip: refs.pop(0) for strip in strips}
        other = {strip: (refs.pop(0), refs.pop(0)) for strip in strips}
        children = own, other, here.core
    return here, make_source(plan, pieces), children, refs


def piece_names(plan, portions, blocks):
    slabs = sorted({block // plan["front_count"] for block in blocks})
    groups = sorted({plan["where"][(p, t)][0] for p in portions for t in slabs})
    return [(group, c) for group in groups for c in (0, 1)]


def leading(plan, state, portions, blocks, strips, space=pltpu.VMEM):
    smem = pl.BlockSpec(memory_space=pltpu.SMEM)
    anywhere = pl.BlockSpec(memory_space=pl.ANY)
    vmem = pl.BlockSpec(memory_space=space)
    operands = [state["routes"]]
    specs = [smem]
    for name in piece_names(plan, portions, blocks):
        operands.append(state["pieces"][name])
        specs.append(anywhere)
    if plan["height"] > 1:
        for strip in strips:
            operands.append(state["own"][strip])
            specs.append(vmem)
        for strip in strips:
            operands.extend(state["other"][strip])
            specs.extend([vmem, vmem])
    return operands, specs


def factor_chunk(plan, state, chunk, factors, inverses):
    low, high = plan["chunks"][chunk]
    size, width = high - low, high
    blocks = range(low // BLK, high // BLK)
    strips = range(low // STRIP, high // STRIP)
    earlier = plan["chunks"][:chunk]

    def kernel(*refs):
        here, source, children, refs = unpack(plan, refs, (0,), blocks, strips)
        old_factors, old_inverses = refs[:chunk], refs[chunk : 2 * chunk]
        factor_ref, inverse_ref, pieces_ref, work_ref, block_ref, spare_ref, sems = refs[2 * chunk :]
        copies = start_copies(plan, here, source, blocks, 0, width, 0, pieces_ref, sems)
        for copy in copies:
            copy.wait()
        if children:
            own, other, core = children
            children = [Child(own, None, core), Child(None, other, core)]
            for order, i in enumerate(blocks):
                for j in range(width // BLK):
                    weights = [
                        here.to_pivot(c, i) * here.to_pivot(c, j) for c in (0, 1)
                    ]
                    pieces_ref[order, :, pl.ds(j * BLK, BLK)] += child_sum(children, i, j, weights)
        rows_ref = pieces_ref.reshape(size, width)
        corner = rows_ref[:, pl.ds(low, size)]
        for index, (first, last) in enumerate(earlier):
            part = rows_ref[:, pl.ds(first, last - first)]
            if index:
                part = part - product_3(
                    factor_ref[:, pl.ds(0, first)], old_factors[index][:, pl.ds(0, first)], True
                )
            part = product_3(part, old_inverses[index][...], True)
            factor_ref[:, pl.ds(first, last - first)] = part
        if chunk:
            done = factor_ref[:, pl.ds(0, low)]
            corner = corner - product_3(done, done, True)
        work_ref[...] = corner
        if width < plan["pivot_size"]:
            factor_ref[:, width:] = jnp.zeros((size, plan["pivot_size"] - width), jnp.float32)
        factor_in_place(work_ref, block_ref, spare_ref, factor_ref, low, inverse_ref)

    operands, specs = leading(plan, state, (0,), blocks, strips)
    vmem = pl.BlockSpec(memory_space=pltpu.VMEM)
    operands += factors[:chunk] + inverses[:chunk]
    specs += [vmem] * (2 * chunk)
    return pl.pallas_call(
        kernel,
        out_shape=[
            jax.ShapeDtypeStruct((size, plan["pivot_size"]), jnp.float32),
            jax.ShapeDtypeStruct((size, size), jnp.float32),
        ],
        in_specs=specs,
        out_specs=[vmem, vmem],
        scratch_shapes=[
            pltpu.VMEM((len(blocks), BLK, width), jnp.float32),
            pltpu.VMEM((size, size), jnp.float32),
            pltpu.VMEM((BLK, BLK), jnp.float32),
            pltpu.VMEM((SUB * (4 * SUB + 2), BLK), jnp.float32),
            pltpu.SemaphoreType.DMA((len(blocks) * 2 ** plan["height"],)),
        ],
        compiler_params=pltpu.CompilerParams(vmem_limit_bytes=(10 + 12 * size // 1024) * 2**20),
        cost_estimate=pl.CostEstimate(
            flops=1, bytes_accessed=1, transcendentals=0
        ),
        name=f"factor_chunk_{chunk}",
    )(*operands)


def panel_and_schur(plan, state, strips, factors, inverses, panel_before, last):
    pivot_size = plan["pivot_size"]
    blocks = range(strips[0] * STRIP // BLK, (strips[-1] + 1) * STRIP // BLK)
    size = len(blocks) * BLK
    start = strips[0] * STRIP
    chunks = plan["chunks"]
    count = len(chunks)
    everything = range(pivot_size // STRIP)
    final = strips[-1] == everything[-1]
    before = [] if panel_before is None else [panel_before]
    first_level = plan["height"] == 1
    rows = plan["piece_rows"]
    slabs = PIVOT_BLOCKS // plan["front_count"]

    def kernel(*refs):
        here, source, children, refs = unpack(plan, refs, (1,), blocks, everything)
        factor_refs, inverse_refs = refs[:count], refs[count : 2 * count]
        refs = refs[2 * count :]
        before_refs, refs = refs[: len(before)], refs[len(before) :]
        panel_ref, refs = refs[0], refs[1:]
        if last:
            schur_refs, refs = refs[:1], refs[1:]
        else:
            schur_refs, refs = refs[: len(strips)], refs[len(strips) :]
        if final:
            own_ref, refs = refs[0], refs[1:]
        pieces_ref, corner3_ref, sems = refs
        rows_ref = pieces_ref.reshape(size, pivot_size)
        corner_ref = corner3_ref.reshape(corner3_ref.shape[0] * BLK, pivot_size)
        copies = start_copies(plan, here, source, blocks, 1, pivot_size, 0, pieces_ref, sems)
        if children:
            own, other, core = children
            children = [Child(own, None, core), Child(None, other, core)]
        for copy in copies:
            copy.wait()
        if children:
            for order, i in enumerate(blocks):
                for j in range(PIVOT_BLOCKS):
                    weights = [
                        (1.0 - here.to_pivot(c, i)) * here.to_pivot(c, j)
                        for c in (0, 1)
                    ]
                    pieces_ref[order, :, pl.ds(j * BLK, BLK)] += child_sum(children, i, j, weights)
                    if last or j // 2 <= i // 2:
                        weights = [
                            (1.0 - here.to_pivot(c, i)) * (1.0 - here.to_pivot(c, j))
                            for c in (0, 1)
                        ]
                        corner3_ref[order, :, pl.ds(j * BLK, BLK)] = child_sum(
                            children, i, j, weights
                        )
        for index, (low, high) in enumerate(chunks):
            part = rows_ref[:, pl.ds(low, high - low)]
            if index:
                part = part - product_3(
                    panel_ref[:, pl.ds(0, low)], factor_refs[index][:, pl.ds(0, low)], True
                )
            panel_ref[:, pl.ds(low, high - low)] = product_3(part, inverse_refs[index][...], True)
        if not last:
            for order, strip in enumerate(strips):
                mine = panel_ref[pl.ds(order * STRIP, STRIP), :]
                for column in range(strip + 1):
                    if column * STRIP < start:
                        other = before_refs[0][pl.ds(column * STRIP, STRIP), :]
                    else:
                        other = panel_ref[pl.ds(column * STRIP - start, STRIP), :]
                    span = pl.ds(column * STRIP, STRIP)
                    value = -product_3(mine, other, True)
                    if not first_level:
                        value = value + corner_ref[pl.ds(order * STRIP, STRIP), span]
                    schur_refs[order][:, span] = value
        if not final:
            return
        piece = pl.multiple_of(here.piece(0) * rows, rows)
        for slab in range(slabs):
            block = here.front + plan["front_count"] * slab
            line = pl.multiple_of(block * BLK + piece, rows)
            for index, (low, high) in enumerate(chunks):

                @pl.when((line >= low) & (line < high))
                def _():
                    own_ref[pl.ds(slab * rows, rows), :] = factor_refs[index][
                        pl.ds(pl.multiple_of(line - low, rows), rows), :
                    ]

            target = pl.ds((slabs + slab) * rows, rows)
            if before:

                @pl.when(line < start)
                def _():
                    own_ref[target, :] = before_refs[0][pl.ds(pl.multiple_of(line, rows), rows), :]

            @pl.when(line >= start)
            def _():
                own_ref[target, :] = panel_ref[pl.ds(pl.multiple_of(line - start, rows), rows), :]

            if last:
                schur_refs[0][pl.ds(slab * rows, rows), :] = corner_ref[pl.ds(line, rows), :]
        if last:
            mine = own_ref[pl.ds(slabs * rows, slabs * rows), :]
            schur_refs[0][...] -= product_3(mine, panel_ref[...], True)

    operands, specs = leading(plan, state, (1,), blocks, everything)
    vmem = pl.BlockSpec(memory_space=pltpu.VMEM)
    operands += factors + inverses + before
    specs += [vmem] * (2 * count + len(before))
    shapes = [(size, pivot_size)]
    if last:
        shapes.append((slabs * rows, pivot_size))
    else:
        shapes += [(STRIP, (strip + 1) * STRIP) for strip in strips]
    if final:
        shapes.append((2 * slabs * rows, pivot_size))
    copy_count = len(blocks) * 2 ** plan["height"]
    return pl.pallas_call(
        kernel,
        out_shape=[jax.ShapeDtypeStruct(shape, jnp.float32) for shape in shapes],
        in_specs=specs,
        out_specs=[vmem] * len(shapes),
        scratch_shapes=[
            pltpu.VMEM((len(blocks), BLK, pivot_size), jnp.float32),
            pltpu.VMEM((1 if first_level else len(blocks), BLK, pivot_size), jnp.float32),
            pltpu.SemaphoreType.DMA((copy_count,)),
        ],
        compiler_params=pltpu.CompilerParams(vmem_limit_bytes=(14 + 16 * size // 1024) * 2**20),
        cost_estimate=pl.CostEstimate(
            flops=1, bytes_accessed=1, transcendentals=0
        ),
        name=f"panel_{strips[0]}",
    )(*operands)


def assemble_rows(plan, routes, entries, kept, received):
    slabs, rows, size = kept.shape
    width = plan["front_count"] * BLK

    def kernel(routes_ref, entries_ref, kept_ref, received_ref, *outs):
        here = Here(plan, routes_ref)
        pivot_refs, (update_ref, left_ref) = outs[:slabs], outs[slabs:]
        columns = [[here.to_pivot(c, j) for c in (0, 1)] for j in range(PIVOT_BLOCKS)]
        for slab in range(slabs):
            line = [here.to_pivot(c, here.front + plan["front_count"] * slab) for c in (0, 1)]
            for j in range(PIVOT_BLOCKS):
                span = pl.ds(j * BLK, BLK)
                parts = (kept_ref[slab, :, span], received_ref[slab, :, span])

                def total(weights):
                    return parts[0] * weights[0] + parts[1] * weights[1]

                if j * BLK < (slab + 1) * width:
                    pivot_refs[slab][:, span] = entries_ref[0, slab, :, span] + total(
                        [line[c] * columns[j][c] for c in (0, 1)]
                    )
                update_ref[slab, :, span] = entries_ref[1, slab, :, span] + total(
                    [(1.0 - line[c]) * columns[j][c] for c in (0, 1)]
                )
                left_ref[slab, :, span] = total(
                    [(1.0 - line[c]) * (1.0 - columns[j][c]) for c in (0, 1)]
                )

    vmem = pl.BlockSpec(memory_space=pltpu.VMEM)
    shapes = [(rows, (slab + 1) * width) for slab in range(slabs)] + [kept.shape] * 2
    outputs = pl.pallas_call(
        kernel,
        out_shape=[jax.ShapeDtypeStruct(shape, jnp.float32) for shape in shapes],
        in_specs=[pl.BlockSpec(memory_space=pltpu.SMEM)] + [vmem] * 3,
        out_specs=[vmem] * len(shapes),
        compiler_params=pltpu.CompilerParams(vmem_limit_bytes=16 * 2**20),
        cost_estimate=pl.CostEstimate(flops=1, bytes_accessed=1, transcendentals=0),
        name="assemble_rows",
    )(routes, entries, kept, received)
    return outputs[:slabs], outputs[slabs], outputs[slabs + 1]


def partner_2(value, axis, stride):
    mask = 2**stride
    pairs = [(source, source ^ mask) for source in range(lax.axis_size(axis))]
    return lax.ppermute(value, axis, pairs)


def all_front(value):
    count = lax.axis_size("front")
    slots = [value]
    for mask in range(1, count):
        pairs = [(source, source ^ mask) for source in range(count)]
        slots.append(lax.ppermute(value, "front", pairs))
    return jnp.stack(slots)


def after(value, done):
    corner = done.reshape(-1)[:1]
    return value + jnp.where(corner > jnp.inf, 1.0, 0.0).reshape((1,) * value.ndim)


def local(
    leaf_contrib,
    entries_lower,
    entries_middle,
    entries_upper,
    assembly_lower,
    assembly_middle,
    assembly_upper,
):
    front_count = lax.axis_size("front")
    slabs = PIVOT_BLOCKS // front_count
    leaf_index = lax.axis_index("leaf")
    pivot_size = leaf_contrib.shape[1]
    core = leaf_index & 1
    chunks = [(0, STRIP), (STRIP, 2 * STRIP), (2 * STRIP, pivot_size)]
    plans, states, entry_slabs = {}, {}, {}
    names = [(p, t) for p in (0, 1) for t in range(slabs)]
    where = {
        1: {(p, t): (slabs, t) if p else (t, None) for p, t in names},
        2: {(p, t): (p, t) for p, t in names},
        3: {(p, t): (1, t) if p else (2 + t, None) for p, t in names},
    }
    direct = {1: (0,), 2: (), 3: ()}
    for height, entries, routes in (
        (1, entries_lower, assembly_lower),
        (2, entries_middle, assembly_middle),
        (3, entries_upper, assembly_upper),
    ):
        piece_rows = BLK // 2**height
        plans[height] = dict(
            height=height,
            piece_rows=piece_rows,
            front_count=front_count,
            pivot_size=pivot_size,
            chunks=chunks,
            where=where[height],
            direct=direct[height],
        )
        states[height] = dict(routes=routes, pieces={})
        entry_slabs[height] = entries.reshape(2, slabs, piece_rows, pivot_size)

    def slab_width(slab):
        return (slab + 1) * front_count * BLK

    def assemble(height, rows):
        half = BLK // 2**height
        child_bit = leaf_index >> height - 1 & 1
        low_rows, high_rows = rows[:, :half], rows[:, half:]
        kept = jnp.where(child_bit == 0, low_rows, high_rows)
        received = partner_2(
            jnp.where(child_bit == 0, high_rows, low_rows), "leaf", height - 1
        )
        return assemble_rows(
            plans[height], states[height]["routes"], entry_slabs[height], kept, received
        )

    lower_pivots, lower_updates, carried = assemble(1, leaf_contrib.reshape(slabs, BLK, pivot_size))

    for height in (2, 3):
        states[height]["own"], states[height]["other"] = {}, {}
    factors = {1: [], 2: [], 3: []}
    inverses = {1: [], 2: [], 3: []}
    now = [leaf_contrib]

    def ready(value):
        return lax.optimization_barrier((value, now[0]))[0]

    def end_step(*results):
        now[0] = results

    def gather(value):
        return lax.all_gather(ready(value), "front")

    def across(value, bit):
        value = ready(value)
        return value, partner_2(value, "leaf", bit)

    def pad_columns(value):
        return jnp.pad(value, ((0, 0), (0, pivot_size - value.shape[1])))

    def joined(pair):
        return jnp.concatenate(pair, axis=0)

    def place(height, group, stack):
        stack = ready(stack)
        pieces = (stack, partner_2(stack, "leaf", 0))
        for index, piece in enumerate(pieces):
            states[height]["pieces"][(group, index)] = piece
        return pieces[1]

    def offer(height, strip):
        half = lax.dynamic_slice_in_dim(states[height]["own"][strip], core * BLK, BLK, 0)
        return partner_2(ready(half), "leaf", height - 1)

    def swap(height, strip, mine):
        theirs = partner_2(ready(mine), "leaf", 0)
        states[height]["other"][strip] = (mine, theirs)
        return theirs

    def factor(height, chunk):
        states[height]["routes"] = ready(states[height]["routes"])
        one, other = factor_chunk(
            plans[height], states[height], chunk, factors[height], inverses[height]
        )
        factors[height].append(one)
        inverses[height].append(other)
        return other

    def panel(height, strips, before, last=False):
        states[height]["routes"] = ready(states[height]["routes"])
        outputs = panel_and_schur(
            plans[height], states[height], strips, factors[height], inverses[height], before, last
        )
        if not last:
            for strip, value in zip(strips, outputs[1:]):
                states[height + 1]["own"][strip] = value
        return outputs

    strips = list(range(pivot_size // STRIP))
    later = range(1, slabs)
    first = all_front(lower_pivots[0])
    end_step(first)
    end_step(place(1, 0, first[None]))

    pivots = [gather(after(lower_pivots[t], first)) for t in later]
    middle_pivots, middle_updates, carried = assemble(2, ready(carried))
    end_step(factor(1, 0), middle_pivots)

    middle = gather(jnp.stack([pad_columns(value) for value in middle_pivots]))
    upper_pivots, upper_updates, carried = assemble(3, ready(carried))
    end_step(factor(1, 1), upper_pivots)

    end_step(*[place(1, t, ready(value)[None]) for t, value in zip(later, pivots)])

    updates = gather(lower_updates)
    end_step(factor(1, 2))

    pair = across(middle[None], 1)
    end_step(pair)
    end_step(place(2, 0, joined(pair)))

    rows = entry_slabs[2].shape[2] // 2
    rest = jnp.concatenate(
        [middle_updates.reshape(-1, rows, pivot_size)]
        + [pad_columns(value)[None] for value in upper_pivots]
        + [upper_updates]
    )
    rest = gather(rest)
    end_step(place(1, slabs, ready(updates)[None]))

    panel_0, _ = panel(1, [0], None)
    end_step(panel_0)

    mine_0 = offer(2, 0)
    panel_rest, _, _, _, lower_own = panel(1, strips[1:], panel_0)
    end_step(panel_rest, mine_0)

    mine_1 = offer(2, 1)
    end_step(swap(2, 0, mine_0))

    mine_2 = offer(2, 2)
    end_step(factor(2, 0), mine_1, mine_2)

    taken = swap(2, 1, mine_1)
    mine_3 = offer(2, 3)
    end_step(taken)

    taken = swap(2, 2, mine_2)
    end_step(factor(2, 1), mine_3, taken)
    end_step(swap(2, 3, mine_3))

    front_count_now = rest.shape[0]
    middle_update = rest[:, : 2 * slabs].reshape(front_count_now, slabs, -1, pivot_size)
    upper = rest[:, 2 * slabs :].reshape(front_count_now, 2, slabs, rows, pivot_size)
    pair = across(middle_update[None], 1)
    upper_pair = across(upper[None], 2)
    end_step(factor(2, 2), pair, upper_pair)

    upper = joined(upper_pair)
    taken = place(2, 1, joined(pair))
    end_step(taken)

    panel_0, _ = panel(2, [0], None)
    end_step(panel_0)

    mine_0 = offer(3, 0)
    pair = across(upper[:, :, 0, 0], 1)
    panel_1, _ = panel(2, [1], panel_0)
    end_step(panel_1, mine_0, pair)

    mine_1 = offer(3, 1)
    taken = swap(3, 0, mine_0), place(3, 2, joined(pair))
    pairs = [across(upper[:, :, 0, t], 1) for t in later]
    before = jnp.concatenate([panel_0, panel_1], axis=0)
    _, _, _, middle_own = panel(2, [2, 3], before)
    end_step(middle_own, mine_1, taken, pairs)

    mine_2, mine_3 = offer(3, 2), offer(3, 3)
    taken = swap(3, 1, mine_1), [place(3, 2 + t, joined(pair)) for t, pair in zip(later, pairs)]
    end_step(factor(3, 0), mine_2, mine_3, taken)

    taken = swap(3, 2, mine_2), swap(3, 3, mine_3)
    end_step(factor(3, 1), taken)

    pair = across(upper[:, :, 1], 1)
    end_step(factor(3, 2), pair)

    end_step(place(3, 1, joined(pair)))
    _, top, upper_own = panel(3, strips, None, True)
    return (lower_own, middle_own, upper_own, top + carried.reshape(-1, pivot_size))


def solution(mesh):
    spec = P(("leaf", "front"), None)
    return jax.shard_map(
        local,
        mesh=mesh,
        in_specs=(spec, spec, spec, spec, P(), P(), P()),
        out_specs=(spec, spec, spec, spec),
        check_vma=False,
    )
```

```python
import jax
import jax.numpy as jnp
from jax import lax
from jax.experimental import pallas as pl
from jax.experimental.pallas import tpu as pltpu
from jax.sharding import PartitionSpec as P

BLK = 128
PIVOT_BLOCKS = 8
SUB = 8
STRIP = 256


def split_parts(value):
    high = value.astype(jnp.bfloat16)
    low = (value - high.astype(jnp.float32)).astype(jnp.bfloat16)
    return high, low


def product_3(left, right, transposed=False):
    dims = (((1,), (1 if transposed else 0,)), ((), ()))
    left_high, left_low = split_parts(left)
    right_high, right_low = split_parts(right)

    def one(first, second):
        return lax.dot_general(first, second, dims, preferred_element_type=jnp.float32)

    return one(left_high, right_high) + (one(left_high, right_low) + one(left_low, right_high))


def invert_block(block, inverse_ref, spare_ref):
    count = BLK // SUB
    shape = (SUB, BLK)
    rows = [block[SUB * m : SUB * m + SUB] for m in range(count)]
    lane = lax.broadcasted_iota(jnp.int32, shape, 1)
    sublane = lax.broadcasted_iota(jnp.int32, shape, 0)

    def columns(m, base):
        return [jnp.broadcast_to(rows[m][:, base + j : base + j + 1], shape) for j in range(SUB)]

    def put(slot, value):
        spare_ref[SUB * slot : SUB * slot + SUB, :] = value

    def get(slot, i):
        return spare_ref[pl.ds(SUB * slot + i, SUB, stride=0), :]

    pivot_slot, next_slot, row_slot = 0, 2 * SUB, 4 * SUB
    for j, value in enumerate(columns(0, 0)):
        put(pivot_slot + j, value)
    for k in range(count):
        base = SUB * k
        turn = k % 2 * SUB
        last = k == count - 1
        d = [[get(pivot_slot + turn + j, i) for j in range(i + 1)] for i in range(SUB)]
        inside = (lane >= base) & (lane < base + SUB)
        unit = (lane == sublane + base).astype(jnp.float32)
        put(row_slot + k % 2, jnp.where(inside, unit, rows[k]))
        y = [get(row_slot + k % 2, j) for j in range(SUB)]
        if not last:
            g = columns(k + 1, base)
            ahead = columns(k + 1, base + SUB)
        f = [[None] * SUB for _ in range(SUB)]
        inverse = [None] * SUB
        for c in range(0, SUB, 2):
            e = c + 1
            p, q, r = d[c][c], d[e][c], d[e][e]
            inverse[c] = 1.0 / p
            both = 1.0 / (p * r - q * q)
            inverse[e] = p * both
            f[e][c] = q * inverse[c]
            h = {}
            for i in range(e + 1, SUB):
                f[i][c] = d[i][c] * inverse[c]
                h[i] = p * d[i][e] - q * d[i][c]
                f[i][e] = h[i] * both
            for i in range(e + 1, SUB):
                w = r * d[i][c] - q * d[i][e]
                for j in range(e + 1, i + 1):
                    d[i][j] = d[i][j] - (w * d[j][c] + h[i] * d[j][e]) * both
            for x in (c, e):
                if not last:
                    put(next_slot + turn + x, g[x])
                    scaled = g[x] * inverse[x]
                    for j in range(SUB):
                        ahead[j] = ahead[j] - scaled * get(next_slot + turn + x, j)
                for i in range(x + 1, SUB):
                    if not last:
                        g[i] = g[i] - f[i][x] * g[x]
                    y[i] = y[i] - f[i][x] * y[x]
        keep = lane[0:1] < base + SUB
        for c in range(SUB):
            row = (lax.rsqrt(inverse[c]) * inverse[c] * y[c])[0:1]
            inverse_ref[base + c : base + c + 1, :] = jnp.where(keep, row, 0.0)
        if last:
            break
        for j in range(SUB):
            put(pivot_slot + SUB - turn + j, ahead[j])
        if k + 2 < count:
            z = [a * b for a, b in zip(y, inverse)]
            for i in reversed(range(SUB)):
                for c in range(i):
                    z[c] = z[c] - f[i][c] * z[i]
        for m in range(k + 1, count):
            cleared = jnp.where(inside, 0.0, rows[m])
            if m == k + 1:
                for c in range(SUB):
                    cleared = cleared - (g[c] * y[c]) * inverse[c]
            else:
                terms = [a * b for a, b in zip(columns(m, base), z)]
                while len(terms) > 1:
                    terms = [a + b for a, b in zip(terms[::2], terms[1::2])]
                cleared = cleared - terms[0]
            rows[m] = cleared


def factor_in_place(work_ref, block_ref, spare_ref, factor_ref, first_column, inverse_ref):
    size = work_ref.shape[0]
    steps = size // BLK
    row = lax.broadcasted_iota(jnp.int32, (BLK, BLK), 0)
    column = lax.broadcasted_iota(jnp.int32, (BLK, BLK), 1)

    def step(index, carry):
        base = pl.multiple_of(index * BLK, BLK)
        invert_block(work_ref[pl.ds(base, BLK), pl.ds(base, BLK)], block_ref, spare_ref)
        for now in range(steps):

            @pl.when(index == now)
            def _():
                low, high = now * BLK, now * BLK + BLK
                block = block_ref[...]
                below = product_3(work_ref[low:, low:high], block, True)
                if now:
                    factor_ref[0:low, first_column + low : first_column + high] = jnp.zeros(
                        (low, BLK), jnp.float32
                    )
                factor_ref[low:high, first_column + low : first_column + high] = jnp.where(
                    row >= column, below[:BLK], 0.0
                )
                inverse_ref[low:high, low:high] = block
                if high < size:
                    inverse_ref[low:high, high:] = jnp.zeros((BLK, size - high), jnp.float32)
                    below = below[BLK:]
                    factor_ref[high:, first_column + low : first_column + high] = below
                    right = product_3(block, work_ref[low:high, high:])
                    work_ref[high:, high:] = work_ref[high:, high:] - product_3(below, right)
                    work_ref[high:, low:high] = -product_3(below, block)
                if now:
                    left = product_3(block, work_ref[low:high, :low])
                    inverse_ref[low:high, :low] = left
                    if high < size:
                        work_ref[high:, :low] = work_ref[high:, :low] - product_3(below, left)

        return carry

    lax.fori_loop(0, steps, step, 0)


class Here:
    def __init__(self, plan, routes_ref):
        height = plan["height"]
        leaf = lax.axis_index("leaf")
        self.front = lax.axis_index("front")
        self.core = leaf & 1
        self.members = leaf & 2**height - 1
        self.height = height
        self.parent = leaf >> height
        self.child = leaf >> height - 1 & 1
        self.routes_ref = routes_ref

    def piece(self, member):
        return reversed_bits(self.members ^ member, self.height)

    def to_pivot(self, child, block):
        route = self.routes_ref[self.parent, self.child ^ child, block]
        return jnp.where(route < PIVOT_BLOCKS, 1.0, 0.0)


def reversed_bits(number, bit_count):
    result = 0
    for bit_index in range(bit_count):
        result = result + (number >> bit_index & 1) * (1 << bit_count - 1 - bit_index)
    return result


def start_copies(plan, here, source, blocks, portion, width, first, target_ref, sems):
    copies = []
    rows = plan["piece_rows"]
    members = 2 ** plan["height"]
    count = plan["front_count"]
    slabs = PIVOT_BLOCKS // count
    blocks = list(blocks)
    for slab in sorted({block // count for block in blocks}):
        fronts = [block % count for block in blocks if block // count == slab]
        order = blocks.index(slab * count + fronts[0])
        group, index = plan["where"][(portion, slab)]
        for member in range(members):
            start = pl.multiple_of(here.piece(member) * rows, rows)
            ref = source(group, member)
            if group in plan["direct"]:
                spans = [(front, 1, here.front ^ front) for front in fronts]
            else:
                spans = [(fronts[0], len(fronts), fronts[0])]
            unit = count * BLK
            cuts = [(first, width, index)]
            if plan["height"] > 1:
                cuts = [
                    (0, min(unit, width - u * unit), index + u) for u in range(-(-width // unit))
                ]
            for front, length, slot in spans:
                at = order + front - fronts[0]
                slots = ref.at[pl.ds(slot, length)]
                for cut, (low, size, part) in enumerate(cuts):
                    chosen = slots if part is None else slots.at[:, part]
                    copy = pltpu.make_async_copy(
                        chosen.at[:, :, pl.ds(low, size)],
                        target_ref.at[pl.ds(at, length), pl.ds(start, rows), pl.ds(cut * unit, size)],
                        sems.at[(at * members + member) * slabs + cut],
                    )
                    copy.start()
                    copies.append(copy)
    return copies


class Child:
    def __init__(self, strips, halves, core):
        self.strips, self.halves, self.core = strips, halves, core

    def block(self, i, j):
        strip, part = i // 2, i % 2
        columns = pl.ds(j * BLK, BLK)
        if self.halves is None:
            return self.strips[strip][pl.ds(part * BLK, BLK), columns]
        mine, theirs = self.halves[strip]
        return jnp.where(self.core == part, mine[:, columns], theirs[:, columns])


def child_sum(children, i, j, weights):
    flip = i // 2 < j // 2
    total = None
    for child, weight in zip(children, weights):
        term = child.block(*((j, i) if flip else (i, j))) * weight
        total = term if total is None else total + term
    return total.T if flip else total


def stack_index(member, height):
    return sum((member >> bit & 1) << height - 1 - bit for bit in range(1, height))


def make_source(plan, refs):
    height = plan["height"]

    def source(group, member):
        return refs[(group, member & 1)].at[stack_index(member, height)]

    return source


def unpack(plan, refs, portions, blocks, strips):
    refs = list(refs)
    here = Here(plan, refs.pop(0))
    names = piece_names(plan, portions, blocks)
    pieces = {name: refs.pop(0) for name in names}
    children = []
    if plan["height"] > 1:
        own = {strip: refs.pop(0) for strip in strips}
        other = {strip: (refs.pop(0), refs.pop(0)) for strip in strips}
        children = own, other, here.core
    return here, make_source(plan, pieces), children, refs


def piece_names(plan, portions, blocks):
    slabs = sorted({block // plan["front_count"] for block in blocks})
    groups = sorted({plan["where"][(p, t)][0] for p in portions for t in slabs})
    return [(group, c) for group in groups for c in (0, 1)]


def leading(plan, state, portions, blocks, strips, space=pltpu.VMEM):
    smem = pl.BlockSpec(memory_space=pltpu.SMEM)
    anywhere = pl.BlockSpec(memory_space=pl.ANY)
    vmem = pl.BlockSpec(memory_space=space)
    operands = [state["routes"]]
    specs = [smem]
    for name in piece_names(plan, portions, blocks):
        operands.append(state["pieces"][name])
        specs.append(anywhere)
    if plan["height"] > 1:
        for strip in strips:
            operands.append(state["own"][strip])
            specs.append(vmem)
        for strip in strips:
            operands.extend(state["other"][strip])
            specs.extend([vmem, vmem])
    return operands, specs


def factor_chunk(plan, state, chunk, factors, inverses):
    low, high = plan["chunks"][chunk]
    size, width = high - low, high
    blocks = range(low // BLK, high // BLK)
    strips = range(low // STRIP, high // STRIP)
    earlier = plan["chunks"][:chunk]

    def kernel(*refs):
        here, source, children, refs = unpack(plan, refs, (0,), blocks, strips)
        old_factors, old_inverses = refs[:chunk], refs[chunk : 2 * chunk]
        factor_ref, inverse_ref, pieces_ref, work_ref, block_ref, spare_ref, sems = refs[2 * chunk :]
        copies = start_copies(plan, here, source, blocks, 0, width, 0, pieces_ref, sems)
        for copy in copies:
            copy.wait()
        if children:
            own, other, core = children
            children = [Child(own, None, core), Child(None, other, core)]
            for order, i in enumerate(blocks):
                for j in range(width // BLK):
                    weights = [
                        here.to_pivot(c, i) * here.to_pivot(c, j) for c in (0, 1)
                    ]
                    pieces_ref[order, :, pl.ds(j * BLK, BLK)] += child_sum(children, i, j, weights)
        rows_ref = pieces_ref.reshape(size, width)
        corner = rows_ref[:, pl.ds(low, size)]
        for index, (first, last) in enumerate(earlier):
            part = rows_ref[:, pl.ds(first, last - first)]
            if index:
                part = part - product_3(
                    factor_ref[:, pl.ds(0, first)], old_factors[index][:, pl.ds(0, first)], True
                )
            part = product_3(part, old_inverses[index][...], True)
            factor_ref[:, pl.ds(first, last - first)] = part
        if chunk:
            done = factor_ref[:, pl.ds(0, low)]
            corner = corner - product_3(done, done, True)
        work_ref[...] = corner
        if width < plan["pivot_size"]:
            factor_ref[:, width:] = jnp.zeros((size, plan["pivot_size"] - width), jnp.float32)
        factor_in_place(work_ref, block_ref, spare_ref, factor_ref, low, inverse_ref)

    operands, specs = leading(plan, state, (0,), blocks, strips)
    vmem = pl.BlockSpec(memory_space=pltpu.VMEM)
    operands += factors[:chunk] + inverses[:chunk]
    specs += [vmem] * (2 * chunk)
    return pl.pallas_call(
        kernel,
        out_shape=[
            jax.ShapeDtypeStruct((size, plan["pivot_size"]), jnp.float32),
            jax.ShapeDtypeStruct((size, size), jnp.float32),
        ],
        in_specs=specs,
        out_specs=[vmem, vmem],
        scratch_shapes=[
            pltpu.VMEM((len(blocks), BLK, width), jnp.float32),
            pltpu.VMEM((size, size), jnp.float32),
            pltpu.VMEM((BLK, BLK), jnp.float32),
            pltpu.VMEM((SUB * (4 * SUB + 2), BLK), jnp.float32),
            pltpu.SemaphoreType.DMA(
                (len(blocks) * 2 ** plan["height"] * PIVOT_BLOCKS // plan["front_count"],)
            ),
        ],
        compiler_params=pltpu.CompilerParams(vmem_limit_bytes=(10 + 12 * size // 1024) * 2**20),
        cost_estimate=pl.CostEstimate(
            flops=1, bytes_accessed=1, transcendentals=0
        ),
        name=f"factor_chunk_{chunk}",
    )(*operands)


def panel_and_schur(plan, state, strips, factors, inverses, panel_before, last):
    pivot_size = plan["pivot_size"]
    blocks = range(strips[0] * STRIP // BLK, (strips[-1] + 1) * STRIP // BLK)
    size = len(blocks) * BLK
    start = strips[0] * STRIP
    chunks = plan["chunks"]
    count = len(chunks)
    everything = range(pivot_size // STRIP)
    final = strips[-1] == everything[-1]
    before = [] if panel_before is None else [panel_before]
    first_level = plan["height"] == 1
    rows = plan["piece_rows"]
    slabs = PIVOT_BLOCKS // plan["front_count"]

    def kernel(*refs):
        here, source, children, refs = unpack(plan, refs, (1,), blocks, everything)
        factor_refs, inverse_refs = refs[:count], refs[count : 2 * count]
        refs = refs[2 * count :]
        before_refs, refs = refs[: len(before)], refs[len(before) :]
        panel_ref, refs = refs[0], refs[1:]
        if last:
            schur_refs, refs = refs[:1], refs[1:]
        else:
            schur_refs, refs = refs[: len(strips)], refs[len(strips) :]
        if final:
            own_ref, refs = refs[0], refs[1:]
        pieces_ref, corner3_ref, sems = refs
        rows_ref = pieces_ref.reshape(size, pivot_size)
        corner_ref = corner3_ref.reshape(corner3_ref.shape[0] * BLK, pivot_size)
        copies = start_copies(plan, here, source, blocks, 1, pivot_size, 0, pieces_ref, sems)
        if children:
            own, other, core = children
            children = [Child(own, None, core), Child(None, other, core)]
        for copy in copies:
            copy.wait()
        if children:
            for order, i in enumerate(blocks):
                for j in range(PIVOT_BLOCKS):
                    weights = [
                        (1.0 - here.to_pivot(c, i)) * here.to_pivot(c, j)
                        for c in (0, 1)
                    ]
                    pieces_ref[order, :, pl.ds(j * BLK, BLK)] += child_sum(children, i, j, weights)
                    if last or j // 2 <= i // 2:
                        weights = [
                            (1.0 - here.to_pivot(c, i)) * (1.0 - here.to_pivot(c, j))
                            for c in (0, 1)
                        ]
                        corner3_ref[order, :, pl.ds(j * BLK, BLK)] = child_sum(
                            children, i, j, weights
                        )
        for index, (low, high) in enumerate(chunks):
            part = rows_ref[:, pl.ds(low, high - low)]
            if index:
                part = part - product_3(
                    panel_ref[:, pl.ds(0, low)], factor_refs[index][:, pl.ds(0, low)], True
                )
            panel_ref[:, pl.ds(low, high - low)] = product_3(part, inverse_refs[index][...], True)
        if not last:
            for order, strip in enumerate(strips):
                mine = panel_ref[pl.ds(order * STRIP, STRIP), :]
                for column in range(strip + 1):
                    if column * STRIP < start:
                        other = before_refs[0][pl.ds(column * STRIP, STRIP), :]
                    else:
                        other = panel_ref[pl.ds(column * STRIP - start, STRIP), :]
                    span = pl.ds(column * STRIP, STRIP)
                    value = -product_3(mine, other, True)
                    if not first_level:
                        value = value + corner_ref[pl.ds(order * STRIP, STRIP), span]
                    schur_refs[order][:, span] = value
        if not final:
            return
        piece = pl.multiple_of(here.piece(0) * rows, rows)
        for slab in range(slabs):
            block = here.front + plan["front_count"] * slab
            line = pl.multiple_of(block * BLK + piece, rows)
            for index, (low, high) in enumerate(chunks):

                @pl.when((line >= low) & (line < high))
                def _():
                    own_ref[pl.ds(slab * rows, rows), :] = factor_refs[index][
                        pl.ds(pl.multiple_of(line - low, rows), rows), :
                    ]

            target = pl.ds((slabs + slab) * rows, rows)
            if before:

                @pl.when(line < start)
                def _():
                    own_ref[target, :] = before_refs[0][pl.ds(pl.multiple_of(line, rows), rows), :]

            @pl.when(line >= start)
            def _():
                own_ref[target, :] = panel_ref[pl.ds(pl.multiple_of(line - start, rows), rows), :]

            if last:
                schur_refs[0][pl.ds(slab * rows, rows), :] = corner_ref[pl.ds(line, rows), :]
        if last:
            mine = own_ref[pl.ds(slabs * rows, slabs * rows), :]
            schur_refs[0][...] -= product_3(mine, panel_ref[...], True)

    operands, specs = leading(plan, state, (1,), blocks, everything)
    vmem = pl.BlockSpec(memory_space=pltpu.VMEM)
    operands += factors + inverses + before
    specs += [vmem] * (2 * count + len(before))
    shapes = [(size, pivot_size)]
    if last:
        shapes.append((slabs * rows, pivot_size))
    else:
        shapes += [(STRIP, (strip + 1) * STRIP) for strip in strips]
    if final:
        shapes.append((2 * slabs * rows, pivot_size))
    copy_count = len(blocks) * 2 ** plan["height"] * slabs
    return pl.pallas_call(
        kernel,
        out_shape=[jax.ShapeDtypeStruct(shape, jnp.float32) for shape in shapes],
        in_specs=specs,
        out_specs=[vmem] * len(shapes),
        scratch_shapes=[
            pltpu.VMEM((len(blocks), BLK, pivot_size), jnp.float32),
            pltpu.VMEM((1 if first_level else len(blocks), BLK, pivot_size), jnp.float32),
            pltpu.SemaphoreType.DMA((copy_count,)),
        ],
        compiler_params=pltpu.CompilerParams(vmem_limit_bytes=(14 + 16 * size // 1024) * 2**20),
        cost_estimate=pl.CostEstimate(
            flops=1, bytes_accessed=1, transcendentals=0
        ),
        name=f"panel_{strips[0]}",
    )(*operands)


def assemble_rows(plan, routes, entries, kept, received):
    slabs, rows, size = kept.shape
    width = plan["front_count"] * BLK

    def kernel(routes_ref, entries_ref, kept_ref, received_ref, *outs):
        here = Here(plan, routes_ref)
        pivot_refs, (update_ref, left_ref) = outs[:slabs], outs[slabs:]
        columns = [[here.to_pivot(c, j) for c in (0, 1)] for j in range(PIVOT_BLOCKS)]
        for slab in range(slabs):
            line = [here.to_pivot(c, here.front + plan["front_count"] * slab) for c in (0, 1)]
            for j in range(PIVOT_BLOCKS):
                span = pl.ds(j * BLK, BLK)
                parts = (kept_ref[slab, :, span], received_ref[slab, :, span])

                def total(weights):
                    return parts[0] * weights[0] + parts[1] * weights[1]

                if j * BLK < (slab + 1) * width:
                    pivot_refs[slab][:, span] = entries_ref[0, slab, :, span] + total(
                        [line[c] * columns[j][c] for c in (0, 1)]
                    )
                update_ref[slab, :, span] = entries_ref[1, slab, :, span] + total(
                    [(1.0 - line[c]) * columns[j][c] for c in (0, 1)]
                )
                left_ref[slab, :, span] = total(
                    [(1.0 - line[c]) * (1.0 - columns[j][c]) for c in (0, 1)]
                )

    vmem = pl.BlockSpec(memory_space=pltpu.VMEM)
    shapes = [(rows, (slab + 1) * width) for slab in range(slabs)] + [kept.shape] * 2
    outputs = pl.pallas_call(
        kernel,
        out_shape=[jax.ShapeDtypeStruct(shape, jnp.float32) for shape in shapes],
        in_specs=[pl.BlockSpec(memory_space=pltpu.SMEM)] + [vmem] * 3,
        out_specs=[vmem] * len(shapes),
        compiler_params=pltpu.CompilerParams(vmem_limit_bytes=16 * 2**20),
        cost_estimate=pl.CostEstimate(flops=1, bytes_accessed=1, transcendentals=0),
        name="assemble_rows",
    )(routes, entries, kept, received)
    return outputs[:slabs], outputs[slabs], outputs[slabs + 1]


def partner_2(value, axis, stride):
    mask = 2**stride
    pairs = [(source, source ^ mask) for source in range(lax.axis_size(axis))]
    return lax.ppermute(value, axis, pairs)


def all_front(value):
    count = lax.axis_size("front")
    slots = [value]
    for mask in range(1, count):
        pairs = [(source, source ^ mask) for source in range(count)]
        slots.append(lax.ppermute(value, "front", pairs))
    return jnp.stack(slots)


def after(value, done):
    corner = done.reshape(-1)[:1]
    return value + jnp.where(corner > jnp.inf, 1.0, 0.0).reshape((1,) * value.ndim)


def local(
    leaf_contrib,
    entries_lower,
    entries_middle,
    entries_upper,
    assembly_lower,
    assembly_middle,
    assembly_upper,
):
    front_count = lax.axis_size("front")
    slabs = PIVOT_BLOCKS // front_count
    leaf_index = lax.axis_index("leaf")
    pivot_size = leaf_contrib.shape[1]
    core = leaf_index & 1
    chunks = [(0, STRIP), (STRIP, 2 * STRIP), (2 * STRIP, pivot_size)]
    plans, states, entry_slabs = {}, {}, {}
    names = [(p, t) for p in (0, 1) for t in range(slabs)]
    where = {
        1: {(p, t): (slabs, t) if p else (t, None) for p, t in names},
        2: {(p, t): (1, t * slabs) if p else (0, t * (t + 1) // 2) for p, t in names},
        3: {(p, t): (1, t * slabs) if p else (2 + t, 0) for p, t in names},
    }
    direct = {1: (0,), 2: (), 3: ()}
    for height, entries, routes in (
        (1, entries_lower, assembly_lower),
        (2, entries_middle, assembly_middle),
        (3, entries_upper, assembly_upper),
    ):
        piece_rows = BLK // 2**height
        plans[height] = dict(
            height=height,
            piece_rows=piece_rows,
            front_count=front_count,
            pivot_size=pivot_size,
            chunks=chunks,
            where=where[height],
            direct=direct[height],
        )
        states[height] = dict(routes=routes, pieces={})
        entry_slabs[height] = entries.reshape(2, slabs, piece_rows, pivot_size)

    def slab_width(slab):
        return (slab + 1) * front_count * BLK

    def assemble(height, rows):
        half = BLK // 2**height
        child_bit = leaf_index >> height - 1 & 1
        low_rows, high_rows = rows[:, :half], rows[:, half:]
        kept = jnp.where(child_bit == 0, low_rows, high_rows)
        received = partner_2(
            jnp.where(child_bit == 0, high_rows, low_rows), "leaf", height - 1
        )
        return assemble_rows(
            plans[height], states[height]["routes"], entry_slabs[height], kept, received
        )

    lower_pivots, lower_updates, carried = assemble(1, leaf_contrib.reshape(slabs, BLK, pivot_size))

    for height in (2, 3):
        states[height]["own"], states[height]["other"] = {}, {}
    factors = {1: [], 2: [], 3: []}
    inverses = {1: [], 2: [], 3: []}
    now = [leaf_contrib]

    def ready(value):
        return lax.optimization_barrier((value, now[0]))[0]

    def end_step(*results):
        now[0] = results

    def gather(value):
        return lax.all_gather(ready(value), "front")

    def across(value, bit):
        value = ready(value)
        return value, partner_2(value, "leaf", bit)

    unit = front_count * BLK

    def units(value):
        return [value[:, low : low + unit] for low in range(0, value.shape[1], unit)]

    def joined(pair):
        return jnp.concatenate(pair, axis=0)

    def place(height, group, stack):
        stack = ready(stack)
        pieces = (stack, partner_2(stack, "leaf", 0))
        for index, piece in enumerate(pieces):
            states[height]["pieces"][(group, index)] = piece
        return pieces[1]

    def offer(height, strip):
        half = lax.dynamic_slice_in_dim(states[height]["own"][strip], core * BLK, BLK, 0)
        return partner_2(ready(half), "leaf", height - 1)

    def swap(height, strip, mine):
        theirs = partner_2(ready(mine), "leaf", 0)
        states[height]["other"][strip] = (mine, theirs)
        return theirs

    def factor(height, chunk):
        states[height]["routes"] = ready(states[height]["routes"])
        one, other = factor_chunk(
            plans[height], states[height], chunk, factors[height], inverses[height]
        )
        factors[height].append(one)
        inverses[height].append(other)
        return other

    def panel(height, strips, before, last=False):
        states[height]["routes"] = ready(states[height]["routes"])
        outputs = panel_and_schur(
            plans[height], states[height], strips, factors[height], inverses[height], before, last
        )
        if not last:
            for strip, value in zip(strips, outputs[1:]):
                states[height + 1]["own"][strip] = value
        return outputs

    strips = list(range(pivot_size // STRIP))
    later = range(1, slabs)
    first = all_front(lower_pivots[0])
    end_step(first)
    end_step(place(1, 0, first[None]))

    pivots = [gather(after(lower_pivots[t], first)) for t in later]
    middle_pivots, middle_updates, carried = assemble(2, ready(carried))
    end_step(factor(1, 0), middle_pivots)

    lower_units = slabs * (slabs + 1) // 2
    middle = jnp.stack([part for value in middle_pivots for part in units(value)])
    middle = gather(jnp.pad(middle, ((0, slabs * slabs - lower_units), (0, 0), (0, 0))))
    upper_pivots, upper_updates, carried = assemble(3, ready(carried))
    end_step(factor(1, 1), upper_pivots)

    end_step(*[place(1, t, ready(value)[None]) for t, value in zip(later, pivots)])

    updates = gather(lower_updates)
    rows = entry_slabs[2].shape[2] // 2
    rest = [part for value in list(middle_updates) + list(upper_pivots) for part in units(value)]
    rest += [part for value in list(upper_updates) for part in units(value)]
    rest = jnp.concatenate([part.reshape(-1, rows, unit) for part in rest])
    end_step(factor(1, 2), rest)

    pair = across(middle[None, :, :lower_units], 1)
    end_step(pair)
    end_step(place(2, 0, joined(pair)))

    rest = gather(rest)
    end_step(place(1, slabs, ready(updates)[None]))

    panel_0, _ = panel(1, [0], None)
    end_step(panel_0)

    mine_0 = offer(2, 0)
    panel_1, _ = panel(1, [1], panel_0)
    end_step(panel_1, mine_0)

    mine_1 = offer(2, 1)
    taken = swap(2, 0, mine_0)
    before = jnp.concatenate([panel_0, panel_1], axis=0)
    _, _, _, lower_own = panel(1, [2, 3], before)
    end_step(lower_own, mine_1, taken)

    mine_2 = offer(2, 2)
    taken = swap(2, 1, mine_1)
    end_step(factor(2, 0), mine_2, taken)

    mine_3 = offer(2, 3)
    taken = swap(2, 2, mine_2)
    end_step(factor(2, 1), mine_3, taken)
    end_step(swap(2, 3, mine_3))

    square = slabs * slabs
    middle_update = rest[:, : 2 * square].reshape(front_count, square, 2 * rows, unit)
    upper = rest[:, 2 * square :]
    pair = across(middle_update[None], 1)
    upper_pair = across(upper[None], 2)
    end_step(factor(2, 2), pair, upper_pair)

    upper = joined(upper_pair)
    taken = place(2, 1, joined(pair))
    end_step(taken)

    panel_0, _ = panel(2, [0], None)
    end_step(panel_0)

    mine_0 = offer(3, 0)
    pair = across(upper[:, :, :1], 1)
    panel_1, _ = panel(2, [1], panel_0)
    end_step(panel_1, mine_0, pair)

    mine_1 = offer(3, 1)
    taken = swap(3, 0, mine_0), place(3, 2, joined(pair))
    pairs = [across(upper[:, :, t * (t + 1) // 2 : (t + 1) * (t + 2) // 2], 1) for t in later]
    before = jnp.concatenate([panel_0, panel_1], axis=0)
    _, _, _, middle_own = panel(2, [2, 3], before)
    end_step(middle_own, mine_1, taken, pairs)

    mine_2 = offer(3, 2)
    taken = swap(3, 1, mine_1), [place(3, 2 + t, joined(pair)) for t, pair in zip(later, pairs)]
    end_step(factor(3, 0), mine_2, taken)

    mine_3 = offer(3, 3)
    taken = swap(3, 2, mine_2)
    end_step(factor(3, 1), mine_3, taken)
    end_step(swap(3, 3, mine_3))

    pair = across(upper[:, :, lower_units:], 1)
    end_step(factor(3, 2), pair)

    end_step(place(3, 1, joined(pair)))
    _, top, upper_own = panel(3, strips, None, True)
    return (lower_own, middle_own, upper_own, top + carried.reshape(-1, pivot_size))


def solution(mesh):
    spec = P(("leaf", "front"), None)
    return jax.shard_map(
        local,
        mesh=mesh,
        in_specs=(spec, spec, spec, spec, P(), P(), P()),
        out_specs=(spec, spec, spec, spec),
        check_vma=False,
    )
```

```python
import jax
import jax.numpy as jnp
from jax import lax
from jax.experimental import pallas as pl
from jax.experimental.pallas import tpu as pltpu
from jax.sharding import PartitionSpec as P

BLK = 128
PIVOT_BLOCKS = 8
SUB = 8
STRIP = 256


def split_parts(value):
    high = value.astype(jnp.bfloat16)
    low = (value - high.astype(jnp.float32)).astype(jnp.bfloat16)
    return high, low


def product_3(left, right, transposed=False):
    dims = (((1,), (1 if transposed else 0,)), ((), ()))
    left_high, left_low = split_parts(left)
    right_high, right_low = split_parts(right)

    def one(first, second):
        return lax.dot_general(first, second, dims, preferred_element_type=jnp.float32)

    return one(left_high, right_high) + (one(left_high, right_low) + one(left_low, right_high))


def invert_block(block, inverse_ref, spare_ref):
    count = BLK // SUB
    shape = (SUB, BLK)
    rows = [block[SUB * m : SUB * m + SUB] for m in range(count)]
    lane = lax.broadcasted_iota(jnp.int32, shape, 1)
    sublane = lax.broadcasted_iota(jnp.int32, shape, 0)

    def columns(m, base):
        return [jnp.broadcast_to(rows[m][:, base + j : base + j + 1], shape) for j in range(SUB)]

    def put(slot, value):
        spare_ref[SUB * slot : SUB * slot + SUB, :] = value

    def get(slot, i):
        return spare_ref[pl.ds(SUB * slot + i, SUB, stride=0), :]

    pivot_slot, next_slot, row_slot = 0, 2 * SUB, 4 * SUB
    for j, value in enumerate(columns(0, 0)):
        put(pivot_slot + j, value)
    for k in range(count):
        base = SUB * k
        turn = k % 2 * SUB
        last = k == count - 1
        d = [[get(pivot_slot + turn + j, i) for j in range(i + 1)] for i in range(SUB)]
        inside = (lane >= base) & (lane < base + SUB)
        unit = (lane == sublane + base).astype(jnp.float32)
        put(row_slot + k % 2, jnp.where(inside, unit, rows[k]))
        y = [get(row_slot + k % 2, j) for j in range(SUB)]
        if not last:
            g = columns(k + 1, base)
            ahead = columns(k + 1, base + SUB)
        f = [[None] * SUB for _ in range(SUB)]
        inverse = [None] * SUB
        for c in range(0, SUB, 2):
            e = c + 1
            p, q, r = d[c][c], d[e][c], d[e][e]
            inverse[c] = 1.0 / p
            both = 1.0 / (p * r - q * q)
            inverse[e] = p * both
            f[e][c] = q * inverse[c]
            h = {}
            for i in range(e + 1, SUB):
                f[i][c] = d[i][c] * inverse[c]
                h[i] = p * d[i][e] - q * d[i][c]
                f[i][e] = h[i] * both
            for i in range(e + 1, SUB):
                w = r * d[i][c] - q * d[i][e]
                for j in range(e + 1, i + 1):
                    d[i][j] = d[i][j] - (w * d[j][c] + h[i] * d[j][e]) * both
            for x in (c, e):
                if not last:
                    put(next_slot + turn + x, g[x])
                    scaled = g[x] * inverse[x]
                    for j in range(SUB):
                        ahead[j] = ahead[j] - scaled * get(next_slot + turn + x, j)
                for i in range(x + 1, SUB):
                    if not last:
                        g[i] = g[i] - f[i][x] * g[x]
                    y[i] = y[i] - f[i][x] * y[x]
        keep = lane[0:1] < base + SUB
        for c in range(SUB):
            row = (lax.rsqrt(inverse[c]) * inverse[c] * y[c])[0:1]
            inverse_ref[base + c : base + c + 1, :] = jnp.where(keep, row, 0.0)
        if last:
            break
        for j in range(SUB):
            put(pivot_slot + SUB - turn + j, ahead[j])
        if k + 2 < count:
            z = [a * b for a, b in zip(y, inverse)]
            for i in reversed(range(SUB)):
                for c in range(i):
                    z[c] = z[c] - f[i][c] * z[i]
        for m in range(k + 1, count):
            cleared = jnp.where(inside, 0.0, rows[m])
            if m == k + 1:
                for c in range(SUB):
                    cleared = cleared - (g[c] * y[c]) * inverse[c]
            else:
                terms = [a * b for a, b in zip(columns(m, base), z)]
                while len(terms) > 1:
                    terms = [a + b for a, b in zip(terms[::2], terms[1::2])]
                cleared = cleared - terms[0]
            rows[m] = cleared


def factor_in_place(work_ref, block_ref, spare_ref, factor_ref, first_column, inverse_ref):
    size = work_ref.shape[0]
    steps = size // BLK
    row = lax.broadcasted_iota(jnp.int32, (BLK, BLK), 0)
    column = lax.broadcasted_iota(jnp.int32, (BLK, BLK), 1)

    def step(index, carry):
        base = pl.multiple_of(index * BLK, BLK)
        invert_block(work_ref[pl.ds(base, BLK), pl.ds(base, BLK)], block_ref, spare_ref)
        for now in range(steps):

            @pl.when(index == now)
            def _():
                low, high = now * BLK, now * BLK + BLK
                block = block_ref[...]
                below = product_3(work_ref[low:, low:high], block, True)
                if now:
                    factor_ref[0:low, first_column + low : first_column + high] = jnp.zeros(
                        (low, BLK), jnp.float32
                    )
                factor_ref[low:high, first_column + low : first_column + high] = jnp.where(
                    row >= column, below[:BLK], 0.0
                )
                inverse_ref[low:high, low:high] = block
                if high < size:
                    inverse_ref[low:high, high:] = jnp.zeros((BLK, size - high), jnp.float32)
                    below = below[BLK:]
                    factor_ref[high:, first_column + low : first_column + high] = below
                    right = product_3(block, work_ref[low:high, high:])
                    work_ref[high:, high:] = work_ref[high:, high:] - product_3(below, right)
                    work_ref[high:, low:high] = -product_3(below, block)
                if now:
                    left = product_3(block, work_ref[low:high, :low])
                    inverse_ref[low:high, :low] = left
                    if high < size:
                        work_ref[high:, :low] = work_ref[high:, :low] - product_3(below, left)

        return carry

    lax.fori_loop(0, steps, step, 0)


class Here:
    def __init__(self, plan, routes_ref):
        height = plan["height"]
        leaf = lax.axis_index("leaf")
        self.front = lax.axis_index("front")
        self.core = leaf & 1
        self.members = leaf & 2**height - 1
        self.height = height
        self.parent = leaf >> height
        self.child = leaf >> height - 1 & 1
        self.routes_ref = routes_ref

    def piece(self, member):
        return reversed_bits(self.members ^ member, self.height)

    def to_pivot(self, child, block):
        route = self.routes_ref[self.parent, self.child ^ child, block]
        return jnp.where(route < PIVOT_BLOCKS, 1.0, 0.0)


def reversed_bits(number, bit_count):
    result = 0
    for bit_index in range(bit_count):
        result = result + (number >> bit_index & 1) * (1 << bit_count - 1 - bit_index)
    return result


def start_copies(plan, here, source, blocks, portion, width, first, target_ref, sems):
    copies = []
    rows = plan["piece_rows"]
    members = 2 ** plan["height"]
    count = plan["front_count"]
    slabs = PIVOT_BLOCKS // count
    blocks = list(blocks)
    for slab in sorted({block // count for block in blocks}):
        fronts = [block % count for block in blocks if block // count == slab]
        order = blocks.index(slab * count + fronts[0])
        group, index = plan["where"][(portion, slab)]
        for member in range(members):
            start = pl.multiple_of(here.piece(member) * rows, rows)
            ref = source(group, member)
            if group in plan["direct"]:
                spans = [(front, 1, here.front ^ front) for front in fronts]
            else:
                spans = [(fronts[0], len(fronts), fronts[0])]
            unit = count * BLK
            cuts = [(first, width, index)]
            if plan["height"] > 1:
                cuts = [
                    (0, min(unit, width - u * unit), index + u) for u in range(-(-width // unit))
                ]
            for front, length, slot in spans:
                at = order + front - fronts[0]
                slots = ref.at[pl.ds(slot, length)]
                for cut, (low, size, part) in enumerate(cuts):
                    chosen = slots if part is None else slots.at[:, part]
                    copy = pltpu.make_async_copy(
                        chosen.at[:, :, pl.ds(low, size)],
                        target_ref.at[pl.ds(at, length), pl.ds(start, rows), pl.ds(cut * unit, size)],
                        sems.at[(at * members + member) * slabs + cut],
                    )
                    copy.start()
                    copies.append(copy)
    return copies


class Child:
    def __init__(self, strips, halves, core):
        self.strips, self.halves, self.core = strips, halves, core

    def block(self, i, j):
        strip, part = i // 2, i % 2
        columns = pl.ds(j * BLK, BLK)
        if self.halves is None:
            return self.strips[strip][pl.ds(part * BLK, BLK), columns]
        mine, theirs = self.halves[strip]
        return jnp.where(self.core == part, mine[:, columns], theirs[:, columns])


def child_sum(children, i, j, weights):
    flip = i // 2 < j // 2
    total = None
    for child, weight in zip(children, weights):
        term = child.block(*((j, i) if flip else (i, j))) * weight
        total = term if total is None else total + term
    return total.T if flip else total


def stack_index(member, height):
    return sum((member >> bit & 1) << height - 1 - bit for bit in range(1, height))


def make_source(plan, refs):
    height = plan["height"]

    def source(group, member):
        return refs[(group, member & 1)].at[stack_index(member, height)]

    return source


def unpack(plan, refs, portions, blocks, strips):
    refs = list(refs)
    here = Here(plan, refs.pop(0))
    names = piece_names(plan, portions, blocks)
    pieces = {name: refs.pop(0) for name in names}
    children = []
    if plan["height"] > 1:
        own = {strip: refs.pop(0) for strip in strips}
        other = {strip: (refs.pop(0), refs.pop(0)) for strip in strips}
        children = own, other, here.core
    return here, make_source(plan, pieces), children, refs


def piece_names(plan, portions, blocks):
    slabs = sorted({block // plan["front_count"] for block in blocks})
    groups = sorted({plan["where"][(p, t)][0] for p in portions for t in slabs})
    return [(group, c) for group in groups for c in (0, 1)]


def leading(plan, state, portions, blocks, strips, space=pltpu.VMEM):
    smem = pl.BlockSpec(memory_space=pltpu.SMEM)
    anywhere = pl.BlockSpec(memory_space=pl.ANY)
    vmem = pl.BlockSpec(memory_space=space)
    operands = [state["routes"]]
    specs = [smem]
    for name in piece_names(plan, portions, blocks):
        operands.append(state["pieces"][name])
        specs.append(anywhere)
    if plan["height"] > 1:
        for strip in strips:
            operands.append(state["own"][strip])
            specs.append(vmem)
        for strip in strips:
            operands.extend(state["other"][strip])
            specs.extend([vmem, vmem])
    return operands, specs


def factor_chunk(plan, state, chunk, factors, inverses):
    low, high = plan["chunks"][chunk]
    size, width = high - low, high
    blocks = range(low // BLK, high // BLK)
    strips = range(low // STRIP, high // STRIP)
    earlier = plan["chunks"][:chunk]

    def kernel(*refs):
        here, source, children, refs = unpack(plan, refs, (0,), blocks, strips)
        old_factors, old_inverses = refs[:chunk], refs[chunk : 2 * chunk]
        factor_ref, inverse_ref, pieces_ref, work_ref, block_ref, spare_ref, sems = refs[2 * chunk :]
        copies = start_copies(plan, here, source, blocks, 0, width, 0, pieces_ref, sems)
        for copy in copies:
            copy.wait()
        if children:
            own, other, core = children
            children = [Child(own, None, core), Child(None, other, core)]
            for order, i in enumerate(blocks):
                for j in range(width // BLK):
                    weights = [
                        here.to_pivot(c, i) * here.to_pivot(c, j) for c in (0, 1)
                    ]
                    pieces_ref[order, :, pl.ds(j * BLK, BLK)] += child_sum(children, i, j, weights)
        rows_ref = pieces_ref.reshape(size, width)
        corner = rows_ref[:, pl.ds(low, size)]
        for index, (first, last) in enumerate(earlier):
            part = rows_ref[:, pl.ds(first, last - first)]
            if index:
                part = part - product_3(
                    factor_ref[:, pl.ds(0, first)], old_factors[index][:, pl.ds(0, first)], True
                )
            part = product_3(part, old_inverses[index][...], True)
            factor_ref[:, pl.ds(first, last - first)] = part
        if chunk:
            done = factor_ref[:, pl.ds(0, low)]
            corner = corner - product_3(done, done, True)
        work_ref[...] = corner
        if width < plan["pivot_size"]:
            factor_ref[:, width:] = jnp.zeros((size, plan["pivot_size"] - width), jnp.float32)
        factor_in_place(work_ref, block_ref, spare_ref, factor_ref, low, inverse_ref)

    operands, specs = leading(plan, state, (0,), blocks, strips)
    vmem = pl.BlockSpec(memory_space=pltpu.VMEM)
    operands += factors[:chunk] + inverses[:chunk]
    specs += [vmem] * (2 * chunk)
    return pl.pallas_call(
        kernel,
        out_shape=[
            jax.ShapeDtypeStruct((size, plan["pivot_size"]), jnp.float32),
            jax.ShapeDtypeStruct((size, size), jnp.float32),
        ],
        in_specs=specs,
        out_specs=[vmem, vmem],
        scratch_shapes=[
            pltpu.VMEM((len(blocks), BLK, width), jnp.float32),
            pltpu.VMEM((size, size), jnp.float32),
            pltpu.VMEM((BLK, BLK), jnp.float32),
            pltpu.VMEM((SUB * (4 * SUB + 2), BLK), jnp.float32),
            pltpu.SemaphoreType.DMA(
                (len(blocks) * 2 ** plan["height"] * PIVOT_BLOCKS // plan["front_count"],)
            ),
        ],
        compiler_params=pltpu.CompilerParams(vmem_limit_bytes=(8 + 8 * size // 1024) * 2**20),
        cost_estimate=pl.CostEstimate(
            flops=1, bytes_accessed=1, transcendentals=0
        ),
        name=f"factor_chunk_{chunk}",
    )(*operands)


def panel_and_schur(plan, state, strips, factors, inverses, panel_before, last):
    pivot_size = plan["pivot_size"]
    blocks = range(strips[0] * STRIP // BLK, (strips[-1] + 1) * STRIP // BLK)
    size = len(blocks) * BLK
    start = strips[0] * STRIP
    chunks = plan["chunks"]
    count = len(chunks)
    everything = range(pivot_size // STRIP)
    final = strips[-1] == everything[-1]
    before = [] if panel_before is None else [panel_before]
    first_level = plan["height"] == 1
    rows = plan["piece_rows"]
    slabs = PIVOT_BLOCKS // plan["front_count"]

    def kernel(*refs):
        here, source, children, refs = unpack(plan, refs, (1,), blocks, everything)
        factor_refs, inverse_refs = refs[:count], refs[count : 2 * count]
        refs = refs[2 * count :]
        before_refs, refs = refs[: len(before)], refs[len(before) :]
        panel_ref, refs = refs[0], refs[1:]
        if last:
            schur_refs, refs = refs[:1], refs[1:]
        else:
            schur_refs, refs = refs[: len(strips)], refs[len(strips) :]
        if final:
            own_ref, refs = refs[0], refs[1:]
        pieces_ref, corner3_ref, sems = refs
        rows_ref = pieces_ref.reshape(size, pivot_size)
        corner_ref = corner3_ref.reshape(corner3_ref.shape[0] * BLK, pivot_size)
        copies = start_copies(plan, here, source, blocks, 1, pivot_size, 0, pieces_ref, sems)
        if children:
            own, other, core = children
            children = [Child(own, None, core), Child(None, other, core)]
        for copy in copies:
            copy.wait()
        if children:
            for order, i in enumerate(blocks):
                for j in range(PIVOT_BLOCKS):
                    weights = [
                        (1.0 - here.to_pivot(c, i)) * here.to_pivot(c, j)
                        for c in (0, 1)
                    ]
                    pieces_ref[order, :, pl.ds(j * BLK, BLK)] += child_sum(children, i, j, weights)
                    if last or j // 2 <= i // 2:
                        weights = [
                            (1.0 - here.to_pivot(c, i)) * (1.0 - here.to_pivot(c, j))
                            for c in (0, 1)
                        ]
                        corner3_ref[order, :, pl.ds(j * BLK, BLK)] = child_sum(
                            children, i, j, weights
                        )
        for index, (low, high) in enumerate(chunks):
            part = rows_ref[:, pl.ds(low, high - low)]
            if index:
                part = part - product_3(
                    panel_ref[:, pl.ds(0, low)], factor_refs[index][:, pl.ds(0, low)], True
                )
            panel_ref[:, pl.ds(low, high - low)] = product_3(part, inverse_refs[index][...], True)
        if not last:
            for order, strip in enumerate(strips):
                mine = panel_ref[pl.ds(order * STRIP, STRIP), :]
                for column in range(strip + 1):
                    if column * STRIP < start:
                        other = before_refs[0][pl.ds(column * STRIP, STRIP), :]
                    else:
                        other = panel_ref[pl.ds(column * STRIP - start, STRIP), :]
                    span = pl.ds(column * STRIP, STRIP)
                    value = -product_3(mine, other, True)
                    if not first_level:
                        value = value + corner_ref[pl.ds(order * STRIP, STRIP), span]
                    schur_refs[order][:, span] = value
        if not final:
            return
        piece = pl.multiple_of(here.piece(0) * rows, rows)
        for slab in range(slabs):
            block = here.front + plan["front_count"] * slab
            line = pl.multiple_of(block * BLK + piece, rows)
            for index, (low, high) in enumerate(chunks):

                @pl.when((line >= low) & (line < high))
                def _():
                    own_ref[pl.ds(slab * rows, rows), :] = factor_refs[index][
                        pl.ds(pl.multiple_of(line - low, rows), rows), :
                    ]

            target = pl.ds((slabs + slab) * rows, rows)
            if before:

                @pl.when(line < start)
                def _():
                    own_ref[target, :] = before_refs[0][pl.ds(pl.multiple_of(line, rows), rows), :]

            @pl.when(line >= start)
            def _():
                own_ref[target, :] = panel_ref[pl.ds(pl.multiple_of(line - start, rows), rows), :]

            if last:
                schur_refs[0][pl.ds(slab * rows, rows), :] = corner_ref[pl.ds(line, rows), :]
        if last:
            mine = own_ref[pl.ds(slabs * rows, slabs * rows), :]
            schur_refs[0][...] -= product_3(mine, panel_ref[...], True)

    operands, specs = leading(plan, state, (1,), blocks, everything)
    vmem = pl.BlockSpec(memory_space=pltpu.VMEM)
    operands += factors + inverses + before
    specs += [vmem] * (2 * count + len(before))
    shapes = [(size, pivot_size)]
    if last:
        shapes.append((slabs * rows, pivot_size))
    else:
        shapes += [(STRIP, (strip + 1) * STRIP) for strip in strips]
    if final:
        shapes.append((2 * slabs * rows, pivot_size))
    copy_count = len(blocks) * 2 ** plan["height"] * slabs
    return pl.pallas_call(
        kernel,
        out_shape=[jax.ShapeDtypeStruct(shape, jnp.float32) for shape in shapes],
        in_specs=specs,
        out_specs=[vmem] * len(shapes),
        scratch_shapes=[
            pltpu.VMEM((len(blocks), BLK, pivot_size), jnp.float32),
            pltpu.VMEM((1 if first_level else len(blocks), BLK, pivot_size), jnp.float32),
            pltpu.SemaphoreType.DMA((copy_count,)),
        ],
        compiler_params=pltpu.CompilerParams(vmem_limit_bytes=(8 + 16 * size // 1024) * 2**20),
        cost_estimate=pl.CostEstimate(
            flops=1, bytes_accessed=1, transcendentals=0
        ),
        name=f"panel_{strips[0]}",
    )(*operands)


def assemble_rows(plan, routes, entries, kept, received):
    slabs, rows, size = kept.shape
    width = plan["front_count"] * BLK

    def kernel(routes_ref, entries_ref, kept_ref, received_ref, *outs):
        here = Here(plan, routes_ref)
        pivot_refs, (update_ref, left_ref) = outs[:slabs], outs[slabs:]
        columns = [[here.to_pivot(c, j) for c in (0, 1)] for j in range(PIVOT_BLOCKS)]
        for slab in range(slabs):
            line = [here.to_pivot(c, here.front + plan["front_count"] * slab) for c in (0, 1)]
            for j in range(PIVOT_BLOCKS):
                span = pl.ds(j * BLK, BLK)
                parts = (kept_ref[slab, :, span], received_ref[slab, :, span])

                def total(weights):
                    return parts[0] * weights[0] + parts[1] * weights[1]

                if j * BLK < (slab + 1) * width:
                    pivot_refs[slab][:, span] = entries_ref[0, slab, :, span] + total(
                        [line[c] * columns[j][c] for c in (0, 1)]
                    )
                update_ref[slab, :, span] = entries_ref[1, slab, :, span] + total(
                    [(1.0 - line[c]) * columns[j][c] for c in (0, 1)]
                )
                left_ref[slab, :, span] = total(
                    [(1.0 - line[c]) * (1.0 - columns[j][c]) for c in (0, 1)]
                )

    vmem = pl.BlockSpec(memory_space=pltpu.VMEM)
    shapes = [(rows, (slab + 1) * width) for slab in range(slabs)] + [kept.shape] * 2
    outputs = pl.pallas_call(
        kernel,
        out_shape=[jax.ShapeDtypeStruct(shape, jnp.float32) for shape in shapes],
        in_specs=[pl.BlockSpec(memory_space=pltpu.SMEM)] + [vmem] * 3,
        out_specs=[vmem] * len(shapes),
        compiler_params=pltpu.CompilerParams(vmem_limit_bytes=16 * 2**20),
        cost_estimate=pl.CostEstimate(flops=1, bytes_accessed=1, transcendentals=0),
        name="assemble_rows",
    )(routes, entries, kept, received)
    return outputs[:slabs], outputs[slabs], outputs[slabs + 1]


def partner_2(value, axis, stride):
    mask = 2**stride
    pairs = [(source, source ^ mask) for source in range(lax.axis_size(axis))]
    return lax.ppermute(value, axis, pairs)


def all_front(value):
    count = lax.axis_size("front")
    slots = [value]
    for mask in range(1, count):
        pairs = [(source, source ^ mask) for source in range(count)]
        slots.append(lax.ppermute(value, "front", pairs))
    return jnp.stack(slots)


def after(value, done):
    corner = done.reshape(-1)[:1]
    return value + jnp.where(corner > jnp.inf, 1.0, 0.0).reshape((1,) * value.ndim)


def local(
    leaf_contrib,
    entries_lower,
    entries_middle,
    entries_upper,
    assembly_lower,
    assembly_middle,
    assembly_upper,
):
    front_count = lax.axis_size("front")
    slabs = PIVOT_BLOCKS // front_count
    leaf_index = lax.axis_index("leaf")
    pivot_size = leaf_contrib.shape[1]
    core = leaf_index & 1
    chunks = [(0, STRIP), (STRIP, 2 * STRIP), (2 * STRIP, pivot_size)]
    plans, states, entry_slabs = {}, {}, {}
    names = [(p, t) for p in (0, 1) for t in range(slabs)]
    where = {
        1: {(p, t): (slabs, t) if p else (t, None) for p, t in names},
        2: {(p, t): (1, t * slabs) if p else (0, t * (t + 1) // 2) for p, t in names},
        3: {(p, t): (p * slabs + t, 0) for p, t in names},
    }
    direct = {1: (0,), 2: (), 3: ()}
    for height, entries, routes in (
        (1, entries_lower, assembly_lower),
        (2, entries_middle, assembly_middle),
        (3, entries_upper, assembly_upper),
    ):
        piece_rows = BLK // 2**height
        plans[height] = dict(
            height=height,
            piece_rows=piece_rows,
            front_count=front_count,
            pivot_size=pivot_size,
            chunks=chunks,
            where=where[height],
            direct=direct[height],
        )
        states[height] = dict(routes=routes, pieces={})
        entry_slabs[height] = entries.reshape(2, slabs, piece_rows, pivot_size)

    def slab_width(slab):
        return (slab + 1) * front_count * BLK

    def assemble(height, rows):
        half = BLK // 2**height
        child_bit = leaf_index >> height - 1 & 1
        low_rows, high_rows = rows[:, :half], rows[:, half:]
        kept = jnp.where(child_bit == 0, low_rows, high_rows)
        received = partner_2(
            jnp.where(child_bit == 0, high_rows, low_rows), "leaf", height - 1
        )
        return assemble_rows(
            plans[height], states[height]["routes"], entry_slabs[height], kept, received
        )

    lower_pivots, lower_updates, carried = assemble(1, leaf_contrib.reshape(slabs, BLK, pivot_size))

    for height in (2, 3):
        states[height]["own"], states[height]["other"] = {}, {}
    factors = {1: [], 2: [], 3: []}
    inverses = {1: [], 2: [], 3: []}
    now = [leaf_contrib]

    def ready(value):
        return lax.optimization_barrier((value, now[0]))[0]

    def end_step(*results):
        now[0] = results

    def gather(value):
        return lax.all_gather(ready(value), "front")

    def across(value, bit):
        value = ready(value)
        return value, partner_2(value, "leaf", bit)

    unit = front_count * BLK

    def units(value):
        return [value[:, low : low + unit] for low in range(0, value.shape[1], unit)]

    def joined(pair):
        return jnp.concatenate(pair, axis=0)

    def place(height, group, stack):
        stack = ready(stack)
        pieces = (stack, partner_2(stack, "leaf", 0))
        for index, piece in enumerate(pieces):
            states[height]["pieces"][(group, index)] = piece
        return pieces[1]

    def offer(height, strip):
        half = lax.dynamic_slice_in_dim(states[height]["own"][strip], core * BLK, BLK, 0)
        return partner_2(ready(half), "leaf", height - 1)

    def swap(height, strip, mine):
        theirs = partner_2(ready(mine), "leaf", 0)
        states[height]["other"][strip] = (mine, theirs)
        return theirs

    def factor(height, chunk):
        states[height]["routes"] = ready(states[height]["routes"])
        one, other = factor_chunk(
            plans[height], states[height], chunk, factors[height], inverses[height]
        )
        factors[height].append(one)
        inverses[height].append(other)
        return other

    def panel(height, strips, before, last=False):
        states[height]["routes"] = ready(states[height]["routes"])
        outputs = panel_and_schur(
            plans[height], states[height], strips, factors[height], inverses[height], before, last
        )
        if not last:
            for strip, value in zip(strips, outputs[1:]):
                states[height + 1]["own"][strip] = value
        return outputs

    strips = list(range(pivot_size // STRIP))
    later = range(1, slabs)
    first = all_front(lower_pivots[0])
    end_step(first)
    end_step(place(1, 0, first[None]))

    pivots = [gather(after(lower_pivots[t], first)) for t in later]
    middle_pivots, middle_updates, carried = assemble(2, ready(carried))
    end_step(factor(1, 0), middle_pivots)

    lower_units = slabs * (slabs + 1) // 2
    middle = jnp.stack([part for value in middle_pivots for part in units(value)])
    middle = gather(jnp.pad(middle, ((0, slabs * slabs - lower_units), (0, 0), (0, 0))))
    upper_pivots, upper_updates, carried = assemble(3, ready(carried))
    end_step(factor(1, 1), upper_pivots)

    end_step(*[place(1, t, ready(value)[None]) for t, value in zip(later, pivots)])

    updates = gather(lower_updates)
    rows = entry_slabs[2].shape[2] // 2
    rest = [part for value in list(middle_updates) + list(upper_pivots) for part in units(value)]
    rest += [part for value in list(upper_updates) for part in units(value)]
    rest = jnp.concatenate([part.reshape(-1, rows, unit) for part in rest])
    end_step(factor(1, 2), rest)

    pair = across(middle[None, :, :lower_units], 1)
    end_step(pair)
    end_step(place(2, 0, joined(pair)))

    rest = gather(rest)
    end_step(place(1, slabs, ready(updates)[None]))

    panel_0, _ = panel(1, [0], None)
    end_step(panel_0)

    mine_0 = offer(2, 0)
    panel_1, _ = panel(1, [1], panel_0)
    end_step(panel_1, mine_0)

    mine_1 = offer(2, 1)
    taken = swap(2, 0, mine_0)
    before = jnp.concatenate([panel_0, panel_1], axis=0)
    _, _, _, lower_own = panel(1, [2, 3], before)
    end_step(lower_own, mine_1, taken)

    mine_2 = offer(2, 2)
    taken = swap(2, 1, mine_1)
    end_step(factor(2, 0), mine_2, taken)

    mine_3 = offer(2, 3)
    taken = swap(2, 2, mine_2)
    end_step(factor(2, 1), mine_3, taken)
    end_step(swap(2, 3, mine_3))

    square = slabs * slabs
    middle_update = rest[:, : 2 * square].reshape(front_count, square, 2 * rows, unit)
    upper = rest[:, 2 * square :]
    pair = across(middle_update[None], 1)
    upper_pair = across(upper[None], 2)
    end_step(factor(2, 2), pair, upper_pair)

    upper = joined(upper_pair)
    taken = place(2, 1, joined(pair))
    end_step(taken)

    panel_0, _ = panel(2, [0], None)
    end_step(panel_0)

    mine_0 = offer(3, 0)
    pair = across(upper[:, :, :1], 1)
    panel_1, _ = panel(2, [1], panel_0)
    end_step(panel_1, mine_0, pair)

    mine_1 = offer(3, 1)
    taken = swap(3, 0, mine_0), place(3, 0, joined(pair))
    pairs = [across(upper[:, :, t * (t + 1) // 2 : (t + 1) * (t + 2) // 2], 1) for t in later]
    before = jnp.concatenate([panel_0, panel_1], axis=0)
    _, _, _, middle_own = panel(2, [2, 3], before)
    end_step(middle_own, mine_1, taken, pairs)

    mine_2 = offer(3, 2)
    taken = swap(3, 1, mine_1), [place(3, t, joined(pair)) for t, pair in zip(later, pairs)]
    end_step(factor(3, 0), mine_2, taken)

    def update_part(t):
        first = lower_units + t * slabs
        return across(upper[:, :, first : first + slabs], 1)

    mine_3 = offer(3, 3)
    taken = swap(3, 2, mine_2)
    pair = update_part(0)
    end_step(factor(3, 1), mine_3, taken, pair)
    end_step(swap(3, 3, mine_3))

    taken = place(3, slabs, joined(pair))
    pairs = [update_part(t) for t in later]
    end_step(factor(3, 2), taken, pairs)
    end_step(*[place(3, slabs + t, joined(pair)) for t, pair in zip(later, pairs)])
    _, top, upper_own = panel(3, strips, None, True)
    return (lower_own, middle_own, upper_own, top + carried.reshape(-1, pivot_size))


def solution(mesh):
    spec = P(("leaf", "front"), None)
    return jax.shard_map(
        local,
        mesh=mesh,
        in_specs=(spec, spec, spec, spec, P(), P(), P()),
        out_specs=(spec, spec, spec, spec),
        check_vma=False,
    )
```

```python
import jax
import jax.numpy as jnp
from jax import lax
from jax.experimental import pallas as pl
from jax.experimental.pallas import tpu as pltpu
from jax.sharding import PartitionSpec as P

BLK = 128
PIVOT_BLOCKS = 8
SUB = 8
STRIP = 256


def split_parts(value):
    high = value.astype(jnp.bfloat16)
    low = (value - high.astype(jnp.float32)).astype(jnp.bfloat16)
    return high, low


def product_3(left, right, transposed=False):
    dims = (((1,), (1 if transposed else 0,)), ((), ()))
    left_high, left_low = split_parts(left)
    right_high, right_low = split_parts(right)

    def one(first, second):
        return lax.dot_general(first, second, dims, preferred_element_type=jnp.float32)

    return one(left_high, right_high) + (one(left_high, right_low) + one(left_low, right_high))


def invert_block(block, inverse_ref, spare_ref):
    count = BLK // SUB
    shape = (SUB, BLK)
    rows = [block[SUB * m : SUB * m + SUB] for m in range(count)]
    lane = lax.broadcasted_iota(jnp.int32, shape, 1)
    sublane = lax.broadcasted_iota(jnp.int32, shape, 0)

    def columns(m, base):
        return [jnp.broadcast_to(rows[m][:, base + j : base + j + 1], shape) for j in range(SUB)]

    def put(slot, value):
        spare_ref[SUB * slot : SUB * slot + SUB, :] = value

    def get(slot, i):
        return spare_ref[pl.ds(SUB * slot + i, SUB, stride=0), :]

    pivot_slot, next_slot, row_slot = 0, 2 * SUB, 4 * SUB
    for j, value in enumerate(columns(0, 0)):
        put(pivot_slot + j, value)
    for k in range(count):
        base = SUB * k
        turn = k % 2 * SUB
        last = k == count - 1
        d = [[get(pivot_slot + turn + j, i) for j in range(i + 1)] for i in range(SUB)]
        inside = (lane >= base) & (lane < base + SUB)
        unit = (lane == sublane + base).astype(jnp.float32)
        put(row_slot + k % 2, jnp.where(inside, unit, rows[k]))
        y = [get(row_slot + k % 2, j) for j in range(SUB)]
        if not last:
            g = columns(k + 1, base)
            ahead = columns(k + 1, base + SUB)
        f = [[None] * SUB for _ in range(SUB)]
        inverse = [None] * SUB
        for c in range(0, SUB, 2):
            e = c + 1
            p, q, r = d[c][c], d[e][c], d[e][e]
            inverse[c] = 1.0 / p
            both = 1.0 / (p * r - q * q)
            inverse[e] = p * both
            f[e][c] = q * inverse[c]
            h = {}
            for i in range(e + 1, SUB):
                f[i][c] = d[i][c] * inverse[c]
                h[i] = p * d[i][e] - q * d[i][c]
                f[i][e] = h[i] * both
            for i in range(e + 1, SUB):
                w = r * d[i][c] - q * d[i][e]
                for j in range(e + 1, i + 1):
                    d[i][j] = d[i][j] - (w * d[j][c] + h[i] * d[j][e]) * both
            for x in (c, e):
                if not last:
                    put(next_slot + turn + x, g[x])
                    scaled = g[x] * inverse[x]
                    for j in range(SUB):
                        ahead[j] = ahead[j] - scaled * get(next_slot + turn + x, j)
                for i in range(x + 1, SUB):
                    if not last:
                        g[i] = g[i] - f[i][x] * g[x]
                    y[i] = y[i] - f[i][x] * y[x]
        keep = lane[0:1] < base + SUB
        for c in range(SUB):
            row = (lax.rsqrt(inverse[c]) * inverse[c] * y[c])[0:1]
            inverse_ref[base + c : base + c + 1, :] = jnp.where(keep, row, 0.0)
        if last:
            break
        for j in range(SUB):
            put(pivot_slot + SUB - turn + j, ahead[j])
        if k + 2 < count:
            z = [a * b for a, b in zip(y, inverse)]
            for i in reversed(range(SUB)):
                for c in range(i):
                    z[c] = z[c] - f[i][c] * z[i]
        for m in range(k + 1, count):
            cleared = jnp.where(inside, 0.0, rows[m])
            if m == k + 1:
                for c in range(SUB):
                    cleared = cleared - (g[c] * y[c]) * inverse[c]
            else:
                terms = [a * b for a, b in zip(columns(m, base), z)]
                while len(terms) > 1:
                    terms = [a + b for a, b in zip(terms[::2], terms[1::2])]
                cleared = cleared - terms[0]
            rows[m] = cleared


def factor_in_place(work_ref, block_ref, spare_ref, factor_ref, first_column, inverse_ref):
    size = work_ref.shape[0]
    steps = size // BLK
    row = lax.broadcasted_iota(jnp.int32, (BLK, BLK), 0)
    column = lax.broadcasted_iota(jnp.int32, (BLK, BLK), 1)

    def step(index, carry):
        base = pl.multiple_of(index * BLK, BLK)
        invert_block(work_ref[pl.ds(base, BLK), pl.ds(base, BLK)], block_ref, spare_ref)
        for now in range(steps):

            @pl.when(index == now)
            def _():
                low, high = now * BLK, now * BLK + BLK
                block = block_ref[...]
                below = product_3(work_ref[low:, low:high], block, True)
                if now:
                    factor_ref[0:low, first_column + low : first_column + high] = jnp.zeros(
                        (low, BLK), jnp.float32
                    )
                factor_ref[low:high, first_column + low : first_column + high] = jnp.where(
                    row >= column, below[:BLK], 0.0
                )
                inverse_ref[low:high, low:high] = block
                if high < size:
                    inverse_ref[low:high, high:] = jnp.zeros((BLK, size - high), jnp.float32)
                    below = below[BLK:]
                    factor_ref[high:, first_column + low : first_column + high] = below
                    right = product_3(block, work_ref[low:high, high:])
                    work_ref[high:, high:] = work_ref[high:, high:] - product_3(below, right)
                    work_ref[high:, low:high] = -product_3(below, block)
                if now:
                    left = product_3(block, work_ref[low:high, :low])
                    inverse_ref[low:high, :low] = left
                    if high < size:
                        work_ref[high:, :low] = work_ref[high:, :low] - product_3(below, left)

        return carry

    lax.fori_loop(0, steps, step, 0)


class Here:
    def __init__(self, plan, routes_ref):
        height = plan["height"]
        leaf = lax.axis_index("leaf")
        self.front = lax.axis_index("front")
        self.core = leaf & 1
        self.members = leaf & 2**height - 1
        self.height = height
        self.parent = leaf >> height
        self.child = leaf >> height - 1 & 1
        self.routes_ref = routes_ref

    def piece(self, member):
        return reversed_bits(self.members ^ member, self.height)

    def to_pivot(self, child, block):
        route = self.routes_ref[self.parent, self.child ^ child, block]
        return jnp.where(route < PIVOT_BLOCKS, 1.0, 0.0)


def reversed_bits(number, bit_count):
    result = 0
    for bit_index in range(bit_count):
        result = result + (number >> bit_index & 1) * (1 << bit_count - 1 - bit_index)
    return result


def start_copies(plan, here, source, blocks, portion, width, first, target_ref, sems):
    copies = []
    rows = plan["piece_rows"]
    members = 2 ** plan["height"]
    count = plan["front_count"]
    slabs = PIVOT_BLOCKS // count
    blocks = list(blocks)
    for slab in sorted({block // count for block in blocks}):
        fronts = [block % count for block in blocks if block // count == slab]
        order = blocks.index(slab * count + fronts[0])
        group, index = plan["where"][(portion, slab)]
        for member in range(members):
            start = pl.multiple_of(here.piece(member) * rows, rows)
            ref = source(group, member)
            if group in plan["direct"]:
                spans = [(front, 1, here.front ^ front) for front in fronts]
            else:
                spans = [(fronts[0], len(fronts), fronts[0])]
            unit = count * BLK
            cuts = [(first, width, index)]
            if plan["height"] > 1:
                cuts = [
                    (0, min(unit, width - u * unit), index + u) for u in range(-(-width // unit))
                ]
            for front, length, slot in spans:
                at = order + front - fronts[0]
                slots = ref.at[pl.ds(slot, length)]
                for cut, (low, size, part) in enumerate(cuts):
                    chosen = slots if part is None else slots.at[:, part]
                    copy = pltpu.make_async_copy(
                        chosen.at[:, :, pl.ds(low, size)],
                        target_ref.at[pl.ds(at, length), pl.ds(start, rows), pl.ds(cut * unit, size)],
                        sems.at[(at * members + member) * slabs + cut],
                    )
                    copy.start()
                    copies.append(copy)
    return copies


class Child:
    def __init__(self, strips, halves, core):
        self.strips, self.halves, self.core = strips, halves, core

    def block(self, i, j):
        strip, part = i // 2, i % 2
        columns = pl.ds(j * BLK, BLK)
        if self.halves is None:
            return self.strips[strip][pl.ds(part * BLK, BLK), columns]
        mine, theirs = self.halves[strip]
        return jnp.where(self.core == part, mine[:, columns], theirs[:, columns])


def child_sum(children, i, j, weights):
    flip = i // 2 < j // 2
    total = None
    for child, weight in zip(children, weights):
        term = child.block(*((j, i) if flip else (i, j))) * weight
        total = term if total is None else total + term
    return total.T if flip else total


def stack_index(member, height):
    return sum((member >> bit & 1) << height - 1 - bit for bit in range(1, height))


def make_source(plan, refs):
    height = plan["height"]

    def source(group, member):
        return refs[(group, member & 1)].at[stack_index(member, height)]

    return source


def unpack(plan, refs, portions, blocks, strips):
    refs = list(refs)
    here = Here(plan, refs.pop(0))
    names = piece_names(plan, portions, blocks)
    pieces = {name: refs.pop(0) for name in names}
    children = []
    if plan["height"] > 1:
        own = {strip: refs.pop(0) for strip in strips}
        other = {strip: (refs.pop(0), refs.pop(0)) for strip in strips}
        children = own, other, here.core
    return here, make_source(plan, pieces), children, refs


def piece_names(plan, portions, blocks):
    slabs = sorted({block // plan["front_count"] for block in blocks})
    groups = sorted({plan["where"][(p, t)][0] for p in portions for t in slabs})
    return [(group, c) for group in groups for c in (0, 1)]


def leading(plan, state, portions, blocks, strips, space=pltpu.VMEM):
    smem = pl.BlockSpec(memory_space=pltpu.SMEM)
    anywhere = pl.BlockSpec(memory_space=pl.ANY)
    vmem = pl.BlockSpec(memory_space=space)
    operands = [state["routes"]]
    specs = [smem]
    for name in piece_names(plan, portions, blocks):
        operands.append(state["pieces"][name])
        specs.append(anywhere)
    if plan["height"] > 1:
        for strip in strips:
            operands.append(state["own"][strip])
            specs.append(vmem)
        for strip in strips:
            operands.extend(state["other"][strip])
            specs.extend([vmem, vmem])
    return operands, specs


def factor_chunk(plan, state, chunk, factors, inverses):
    low, high = plan["chunks"][chunk]
    size, width = high - low, high
    blocks = range(low // BLK, high // BLK)
    strips = range(low // STRIP, high // STRIP)
    earlier = plan["chunks"][:chunk]

    def kernel(*refs):
        here, source, children, refs = unpack(plan, refs, (0,), blocks, strips)
        old_factors, old_inverses = refs[:chunk], refs[chunk : 2 * chunk]
        factor_ref, inverse_ref, pieces_ref, work_ref, block_ref, spare_ref, sems = refs[2 * chunk :]
        copies = start_copies(plan, here, source, blocks, 0, width, 0, pieces_ref, sems)
        for copy in copies:
            copy.wait()
        if children:
            own, other, core = children
            children = [Child(own, None, core), Child(None, other, core)]
            for order, i in enumerate(blocks):
                for j in range(width // BLK):
                    weights = [
                        here.to_pivot(c, i) * here.to_pivot(c, j) for c in (0, 1)
                    ]
                    pieces_ref[order, :, pl.ds(j * BLK, BLK)] += child_sum(children, i, j, weights)
        rows_ref = pieces_ref.reshape(size, width)
        corner = rows_ref[:, pl.ds(low, size)]
        for index, (first, last) in enumerate(earlier):
            part = rows_ref[:, pl.ds(first, last - first)]
            if index:
                part = part - product_3(
                    factor_ref[:, pl.ds(0, first)], old_factors[index][:, pl.ds(0, first)], True
                )
            part = product_3(part, old_inverses[index][...], True)
            factor_ref[:, pl.ds(first, last - first)] = part
        if chunk:
            done = factor_ref[:, pl.ds(0, low)]
            corner = corner - product_3(done, done, True)
        work_ref[...] = corner
        if width < plan["pivot_size"]:
            factor_ref[:, width:] = jnp.zeros((size, plan["pivot_size"] - width), jnp.float32)
        factor_in_place(work_ref, block_ref, spare_ref, factor_ref, low, inverse_ref)

    operands, specs = leading(plan, state, (0,), blocks, strips)
    vmem = pl.BlockSpec(memory_space=pltpu.VMEM)
    operands += factors[:chunk] + inverses[:chunk]
    specs += [vmem] * (2 * chunk)
    return pl.pallas_call(
        kernel,
        out_shape=[
            jax.ShapeDtypeStruct((size, plan["pivot_size"]), jnp.float32),
            jax.ShapeDtypeStruct((size, size), jnp.float32),
        ],
        in_specs=specs,
        out_specs=[vmem, vmem],
        scratch_shapes=[
            pltpu.VMEM((len(blocks), BLK, width), jnp.float32),
            pltpu.VMEM((size, size), jnp.float32),
            pltpu.VMEM((BLK, BLK), jnp.float32),
            pltpu.VMEM((SUB * (4 * SUB + 3), BLK), jnp.float32),
            pltpu.SemaphoreType.DMA(
                (len(blocks) * 2 ** plan["height"] * PIVOT_BLOCKS // plan["front_count"],)
            ),
        ],
        compiler_params=pltpu.CompilerParams(vmem_limit_bytes=(8 + 8 * size // 1024) * 2**20),
        cost_estimate=pl.CostEstimate(
            flops=1, bytes_accessed=1, transcendentals=0
        ),
        name=f"factor_chunk_{chunk}",
    )(*operands)


def panel_and_schur(plan, state, strips, factors, inverses, panel_before, last):
    pivot_size = plan["pivot_size"]
    blocks = range(strips[0] * STRIP // BLK, (strips[-1] + 1) * STRIP // BLK)
    size = len(blocks) * BLK
    start = strips[0] * STRIP
    chunks = plan["chunks"]
    count = len(chunks)
    everything = range(pivot_size // STRIP)
    final = strips[-1] == everything[-1]
    before = [] if panel_before is None else [panel_before]
    first_level = plan["height"] == 1
    rows = plan["piece_rows"]
    slabs = PIVOT_BLOCKS // plan["front_count"]

    def kernel(*refs):
        here, source, children, refs = unpack(plan, refs, (1,), blocks, everything)
        factor_refs, inverse_refs = refs[:count], refs[count : 2 * count]
        refs = refs[2 * count :]
        before_refs, refs = refs[: len(before)], refs[len(before) :]
        panel_ref, refs = refs[0], refs[1:]
        if last:
            schur_refs, refs = refs[:1], refs[1:]
        else:
            schur_refs, refs = refs[: len(strips)], refs[len(strips) :]
        if final:
            own_ref, refs = refs[0], refs[1:]
        pieces_ref, corner3_ref, sems = refs
        rows_ref = pieces_ref.reshape(size, pivot_size)
        corner_ref = corner3_ref.reshape(corner3_ref.shape[0] * BLK, pivot_size)
        copies = start_copies(plan, here, source, blocks, 1, pivot_size, 0, pieces_ref, sems)
        if children:
            own, other, core = children
            children = [Child(own, None, core), Child(None, other, core)]
        for copy in copies:
            copy.wait()
        if children:
            for order, i in enumerate(blocks):
                for j in range(PIVOT_BLOCKS):
                    weights = [
                        (1.0 - here.to_pivot(c, i)) * here.to_pivot(c, j)
                        for c in (0, 1)
                    ]
                    pieces_ref[order, :, pl.ds(j * BLK, BLK)] += child_sum(children, i, j, weights)
                    if last or j // 2 <= i // 2:
                        weights = [
                            (1.0 - here.to_pivot(c, i)) * (1.0 - here.to_pivot(c, j))
                            for c in (0, 1)
                        ]
                        corner3_ref[order, :, pl.ds(j * BLK, BLK)] = child_sum(
                            children, i, j, weights
                        )
        for index, (low, high) in enumerate(chunks):
            part = rows_ref[:, pl.ds(low, high - low)]
            if index:
                part = part - product_3(
                    panel_ref[:, pl.ds(0, low)], factor_refs[index][:, pl.ds(0, low)], True
                )
            panel_ref[:, pl.ds(low, high - low)] = product_3(part, inverse_refs[index][...], True)
        if not last:
            for order, strip in enumerate(strips):
                mine = panel_ref[pl.ds(order * STRIP, STRIP), :]
                for column in range(strip + 1):
                    if column * STRIP < start:
                        other = before_refs[0][pl.ds(column * STRIP, STRIP), :]
                    else:
                        other = panel_ref[pl.ds(column * STRIP - start, STRIP), :]
                    span = pl.ds(column * STRIP, STRIP)
                    value = -product_3(mine, other, True)
                    if not first_level:
                        value = value + corner_ref[pl.ds(order * STRIP, STRIP), span]
                    schur_refs[order][:, span] = value
        if not final:
            return
        piece = pl.multiple_of(here.piece(0) * rows, rows)
        for slab in range(slabs):
            block = here.front + plan["front_count"] * slab
            line = pl.multiple_of(block * BLK + piece, rows)
            for index, (low, high) in enumerate(chunks):

                @pl.when((line >= low) & (line < high))
                def _():
                    own_ref[pl.ds(slab * rows, rows), :] = factor_refs[index][
                        pl.ds(pl.multiple_of(line - low, rows), rows), :
                    ]

            target = pl.ds((slabs + slab) * rows, rows)
            if before:

                @pl.when(line < start)
                def _():
                    own_ref[target, :] = before_refs[0][pl.ds(pl.multiple_of(line, rows), rows), :]

            @pl.when(line >= start)
            def _():
                own_ref[target, :] = panel_ref[pl.ds(pl.multiple_of(line - start, rows), rows), :]

            if last:
                schur_refs[0][pl.ds(slab * rows, rows), :] = corner_ref[pl.ds(line, rows), :]
        if last:
            mine = own_ref[pl.ds(slabs * rows, slabs * rows), :]
            schur_refs[0][...] -= product_3(mine, panel_ref[...], True)

    operands, specs = leading(plan, state, (1,), blocks, everything)
    vmem = pl.BlockSpec(memory_space=pltpu.VMEM)
    operands += factors + inverses + before
    specs += [vmem] * (2 * count + len(before))
    shapes = [(size, pivot_size)]
    if last:
        shapes.append((slabs * rows, pivot_size))
    else:
        shapes += [(STRIP, (strip + 1) * STRIP) for strip in strips]
    if final:
        shapes.append((2 * slabs * rows, pivot_size))
    copy_count = len(blocks) * 2 ** plan["height"] * slabs
    return pl.pallas_call(
        kernel,
        out_shape=[jax.ShapeDtypeStruct(shape, jnp.float32) for shape in shapes],
        in_specs=specs,
        out_specs=[vmem] * len(shapes),
        scratch_shapes=[
            pltpu.VMEM((len(blocks), BLK, pivot_size), jnp.float32),
            pltpu.VMEM((1 if first_level else len(blocks), BLK, pivot_size), jnp.float32),
            pltpu.SemaphoreType.DMA((copy_count,)),
        ],
        compiler_params=pltpu.CompilerParams(vmem_limit_bytes=(8 + 16 * size // 1024) * 2**20),
        cost_estimate=pl.CostEstimate(
            flops=1, bytes_accessed=1, transcendentals=0
        ),
        name=f"panel_{strips[0]}",
    )(*operands)


def assemble_rows(plan, routes, entries, kept, received):
    slabs, rows, size = kept.shape
    width = plan["front_count"] * BLK

    def kernel(routes_ref, entries_ref, kept_ref, received_ref, *outs):
        here = Here(plan, routes_ref)
        pivot_refs, (update_ref, left_ref) = outs[:slabs], outs[slabs:]
        columns = [[here.to_pivot(c, j) for c in (0, 1)] for j in range(PIVOT_BLOCKS)]
        for slab in range(slabs):
            line = [here.to_pivot(c, here.front + plan["front_count"] * slab) for c in (0, 1)]
            for j in range(PIVOT_BLOCKS):
                span = pl.ds(j * BLK, BLK)
                parts = (kept_ref[slab, :, span], received_ref[slab, :, span])

                def total(weights):
                    return parts[0] * weights[0] + parts[1] * weights[1]

                if j * BLK < (slab + 1) * width:
                    pivot_refs[slab][:, span] = entries_ref[0, slab, :, span] + total(
                        [line[c] * columns[j][c] for c in (0, 1)]
                    )
                update_ref[slab, :, span] = entries_ref[1, slab, :, span] + total(
                    [(1.0 - line[c]) * columns[j][c] for c in (0, 1)]
                )
                left_ref[slab, :, span] = total(
                    [(1.0 - line[c]) * (1.0 - columns[j][c]) for c in (0, 1)]
                )

    vmem = pl.BlockSpec(memory_space=pltpu.VMEM)
    shapes = [(rows, (slab + 1) * width) for slab in range(slabs)] + [kept.shape] * 2
    outputs = pl.pallas_call(
        kernel,
        out_shape=[jax.ShapeDtypeStruct(shape, jnp.float32) for shape in shapes],
        in_specs=[pl.BlockSpec(memory_space=pltpu.SMEM)] + [vmem] * 3,
        out_specs=[vmem] * len(shapes),
        compiler_params=pltpu.CompilerParams(vmem_limit_bytes=16 * 2**20),
        cost_estimate=pl.CostEstimate(flops=1, bytes_accessed=1, transcendentals=0),
        name="assemble_rows",
    )(routes, entries, kept, received)
    return outputs[:slabs], outputs[slabs], outputs[slabs + 1]


def partner_2(value, axis, stride):
    mask = 2**stride
    pairs = [(source, source ^ mask) for source in range(lax.axis_size(axis))]
    return lax.ppermute(value, axis, pairs)


def all_front(value):
    count = lax.axis_size("front")
    slots = [value]
    for mask in range(1, count):
        pairs = [(source, source ^ mask) for source in range(count)]
        slots.append(lax.ppermute(value, "front", pairs))
    return jnp.stack(slots)


def after(value, done):
    corner = done.reshape(-1)[:1]
    return value + jnp.where(corner > jnp.inf, 1.0, 0.0).reshape((1,) * value.ndim)


def local(
    leaf_contrib,
    entries_lower,
    entries_middle,
    entries_upper,
    assembly_lower,
    assembly_middle,
    assembly_upper,
):
    front_count = lax.axis_size("front")
    slabs = PIVOT_BLOCKS // front_count
    leaf_index = lax.axis_index("leaf")
    pivot_size = leaf_contrib.shape[1]
    core = leaf_index & 1
    chunks = [(0, STRIP), (STRIP, 2 * STRIP), (2 * STRIP, pivot_size)]
    plans, states, entry_slabs = {}, {}, {}
    names = [(p, t) for p in (0, 1) for t in range(slabs)]
    where = {
        1: {(p, t): (slabs, t) if p else (t, None) for p, t in names},
        2: {(p, t): (1, t * slabs) if p else (0, t * (t + 1) // 2) for p, t in names},
        3: {(p, t): (p * slabs + t, 0) for p, t in names},
    }
    direct = {1: (0,), 2: (), 3: ()}
    for height, entries, routes in (
        (1, entries_lower, assembly_lower),
        (2, entries_middle, assembly_middle),
        (3, entries_upper, assembly_upper),
    ):
        piece_rows = BLK // 2**height
        plans[height] = dict(
            height=height,
            piece_rows=piece_rows,
            front_count=front_count,
            pivot_size=pivot_size,
            chunks=chunks,
            where=where[height],
            direct=direct[height],
        )
        states[height] = dict(routes=routes, pieces={})
        entry_slabs[height] = entries.reshape(2, slabs, piece_rows, pivot_size)

    def slab_width(slab):
        return (slab + 1) * front_count * BLK

    def assemble(height, rows):
        half = BLK // 2**height
        child_bit = leaf_index >> height - 1 & 1
        low_rows, high_rows = rows[:, :half], rows[:, half:]
        kept = jnp.where(child_bit == 0, low_rows, high_rows)
        received = partner_2(
            jnp.where(child_bit == 0, high_rows, low_rows), "leaf", height - 1
        )
        return assemble_rows(
            plans[height], states[height]["routes"], entry_slabs[height], kept, received
        )

    lower_pivots, lower_updates, carried = assemble(1, leaf_contrib.reshape(slabs, BLK, pivot_size))

    for height in (2, 3):
        states[height]["own"], states[height]["other"] = {}, {}
    factors = {1: [], 2: [], 3: []}
    inverses = {1: [], 2: [], 3: []}
    now = [leaf_contrib]

    def ready(value):
        return lax.optimization_barrier((value, now[0]))[0]

    def end_step(*results):
        now[0] = results

    def gather(value):
        return lax.all_gather(ready(value), "front")

    def across(value, bit):
        value = ready(value)
        return value, partner_2(value, "leaf", bit)

    unit = front_count * BLK

    def units(value):
        return [value[:, low : low + unit] for low in range(0, value.shape[1], unit)]

    def joined(pair):
        return jnp.concatenate(pair, axis=0)

    def place(height, group, stack):
        stack = ready(stack)
        pieces = (stack, partner_2(stack, "leaf", 0))
        for index, piece in enumerate(pieces):
            states[height]["pieces"][(group, index)] = piece
        return pieces[1]

    def offer(height, strip):
        half = lax.dynamic_slice_in_dim(states[height]["own"][strip], core * BLK, BLK, 0)
        return partner_2(ready(half), "leaf", height - 1)

    def swap(height, strip, mine):
        theirs = partner_2(ready(mine), "leaf", 0)
        states[height]["other"][strip] = (mine, theirs)
        return theirs

    def factor(height, chunk):
        states[height]["routes"] = ready(states[height]["routes"])
        one, other = factor_chunk(
            plans[height], states[height], chunk, factors[height], inverses[height]
        )
        factors[height].append(one)
        inverses[height].append(other)
        return other

    def panel(height, strips, before, last=False):
        states[height]["routes"] = ready(states[height]["routes"])
        outputs = panel_and_schur(
            plans[height], states[height], strips, factors[height], inverses[height], before, last
        )
        if not last:
            for strip, value in zip(strips, outputs[1:]):
                states[height + 1]["own"][strip] = value
        return outputs

    strips = list(range(pivot_size // STRIP))
    later = range(1, slabs)
    first = all_front(lower_pivots[0])
    end_step(first)
    end_step(place(1, 0, first[None]))

    pivots = [gather(after(lower_pivots[t], first)) for t in later]
    middle_pivots, middle_updates, carried = assemble(2, ready(carried))
    end_step(factor(1, 0), middle_pivots)

    lower_units = slabs * (slabs + 1) // 2
    middle = jnp.stack([part for value in middle_pivots for part in units(value)])
    middle = gather(jnp.pad(middle, ((0, slabs * slabs - lower_units), (0, 0), (0, 0))))
    upper_pivots, upper_updates, carried = assemble(3, ready(carried))
    end_step(factor(1, 1), upper_pivots)

    end_step(*[place(1, t, ready(value)[None]) for t, value in zip(later, pivots)])

    updates = gather(lower_updates)
    rows = entry_slabs[2].shape[2] // 2
    rest = [part for value in list(middle_updates) + list(upper_pivots) for part in units(value)]
    rest += [part for value in list(upper_updates) for part in units(value)]
    rest = jnp.concatenate([part.reshape(-1, rows, unit) for part in rest])
    end_step(factor(1, 2), rest)

    pair = across(middle[None, :, :lower_units], 1)
    end_step(pair)
    end_step(place(2, 0, joined(pair)))

    rest = gather(rest)
    end_step(place(1, slabs, ready(updates)[None]))

    panel_0, _ = panel(1, [0], None)
    end_step(panel_0)

    mine_0 = offer(2, 0)
    panel_1, _ = panel(1, [1], panel_0)
    end_step(panel_1, mine_0)

    mine_1 = offer(2, 1)
    taken = swap(2, 0, mine_0)
    before = jnp.concatenate([panel_0, panel_1], axis=0)
    _, _, _, lower_own = panel(1, [2, 3], before)
    end_step(lower_own, mine_1, taken)

    mine_2 = offer(2, 2)
    taken = swap(2, 1, mine_1)
    end_step(factor(2, 0), mine_2, taken)

    mine_3 = offer(2, 3)
    taken = swap(2, 2, mine_2)
    end_step(factor(2, 1), mine_3, taken)
    end_step(swap(2, 3, mine_3))

    square = slabs * slabs
    middle_update = rest[:, : 2 * square].reshape(front_count, square, 2 * rows, unit)
    upper = rest[:, 2 * square :]
    pair = across(middle_update[None], 1)
    upper_pair = across(upper[None], 2)
    end_step(factor(2, 2), pair, upper_pair)

    upper = joined(upper_pair)
    taken = place(2, 1, joined(pair))
    end_step(taken)

    panel_0, _ = panel(2, [0], None)
    end_step(panel_0)

    mine_0 = offer(3, 0)
    pair = across(upper[:, :, :1], 1)
    panel_1, _ = panel(2, [1], panel_0)
    end_step(panel_1, mine_0, pair)

    mine_1 = offer(3, 1)
    taken = swap(3, 0, mine_0), place(3, 0, joined(pair))
    pairs = [across(upper[:, :, t * (t + 1) // 2 : (t + 1) * (t + 2) // 2], 1) for t in later]
    before = jnp.concatenate([panel_0, panel_1], axis=0)
    _, _, _, middle_own = panel(2, [2, 3], before)
    end_step(middle_own, mine_1, taken, pairs)

    mine_2 = offer(3, 2)
    taken = swap(3, 1, mine_1), [place(3, t, joined(pair)) for t, pair in zip(later, pairs)]
    end_step(factor(3, 0), mine_2, taken)

    def update_part(t):
        first = lower_units + t * slabs
        return across(upper[:, :, first : first + slabs], 1)

    mine_3 = offer(3, 3)
    taken = swap(3, 2, mine_2)
    pair = update_part(0)
    end_step(factor(3, 1), mine_3, taken, pair)
    end_step(swap(3, 3, mine_3))

    taken = place(3, slabs, joined(pair))
    pairs = [update_part(t) for t in later]
    end_step(factor(3, 2), taken, pairs)
    end_step(*[place(3, slabs + t, joined(pair)) for t, pair in zip(later, pairs)])
    _, top, upper_own = panel(3, strips, None, True)
    return (lower_own, middle_own, upper_own, top + carried.reshape(-1, pivot_size))


def solution(mesh):
    spec = P(("leaf", "front"), None)
    return jax.shard_map(
        local,
        mesh=mesh,
        in_specs=(spec, spec, spec, spec, P(), P(), P()),
        out_specs=(spec, spec, spec, spec),
        check_vma=False,
    )
```
